256 devices in a mesh: dom: 32 (over y, z), rep: 8 (over x, core).
Axes of the slice: x: 4, y: 4, z: 8, core: 2. Of those that a mesh axis runs over, the one named last changes fastest.
Arguments:
- queries: bfloat16 [16384, 256], P(('dom', 'rep')), may hold values from -80 to 80
- probes: int32 [16384, 8], P(('dom', 'rep')), may hold values from 0 to 63, all different within a row; in each aligned block of 64 rows (0 to 63, 64 to 127, ...) at most 16 rows name the same one
- corpus: bfloat16 [64, 8192, 256], P('dom', 'rep'), may hold values from -20 to 20
- labels: int32 [64, 8192], P('dom', 'rep'), may hold values from 0 to 127
Outputs:
- type_scores: float32 [16384, 128], P(('dom', 'rep'))
The draws below stay inside these ranges and needn't reach their ends.
Inputs may be any that keep to these rules, and one draw needn't show every extreme that they name: `probes`: each query names 8 different partitions. The 64 queries of one device name one partition at most 16 times, a bound that some block reaches.
All inputs are finite; a program needn't handle non-finite values.
Results may differ from the reference program's by a relative error of at most 0.00085.
Values may be sent and summed in bfloat16 or wider, within the bound.
A program may use at most 128 MiB of HBM per device.

```python
import math
import jax
import jax.numpy as jnp
import numpy as np
from jax import lax

D = 256
NCLASS = 128
PROBES = 8
PART_ROWS_DEV = 1024
Q_DEV = 64
NPART = 64
PROWS = 8192
NQ = 16384
CAP = 16
N_REP = 8
DEVICES = 256


def draw_queries(key, part):
    first_key = jax.random.fold_in(key, 21)
    values = jnp.clip(jax.random.normal(first_key, (NQ, D), jnp.float32), -6.0, 6.0)
    return values.astype(jnp.bfloat16)


def draw_corpus(key, part):
    first_key = jax.random.fold_in(key, 31)
    second_key = jax.random.fold_in(key, 32)
    row_scale = jnp.exp(jax.random.uniform(second_key, (NPART, PROWS, 1), jnp.float32, math.log(0.3), math.log(3.0)))
    values = jnp.clip(jax.random.normal(first_key, (NPART, PROWS, D), jnp.float32), -6.0, 6.0) * row_scale
    return values.astype(jnp.bfloat16)


def place_ends(values, rng, least, top_value):
    place = [jax.random.randint(jax.random.fold_in(rng, axis), (), 0, length) for axis, length in enumerate(values.shape)]
    longest = values.shape.index(max(values.shape))
    neighbour = place[:longest] + [(place[longest] + 1) % values.shape[longest]] + place[longest + 1:]
    return values.at[tuple(place)].set(least).at[tuple(neighbour)].set(top_value)


def shared_out(stream_key, own, number, rows, amount, top, most, skew):
    order = jax.random.permutation(stream_key, amount)
    packed, common = shares(amount, rows * top, most, skew, True), shares(amount, rows * top, most, skew, False)
    places = jnp.arange(amount)

    def named(sizes, offset_by):
        used = int((sizes > 0).sum())
        fixed = max(1, used // 4)
        shifted = fixed + (places - fixed + offset_by * (used - fixed)) % max(1, amount - fixed)
        return jnp.zeros((amount,), jnp.int32).at[order[jnp.where(places < fixed, places, shifted)]].set(jnp.asarray(sizes, jnp.int32))

    sizes = jnp.where(number % 4 == 0, named(packed, number // 4), named(common, number - number // 4 - 1))
    mixed = jax.random.permutation(jax.random.fold_in(own, 3), amount)
    donor, sink = mixed[0:amount // 2 * 2:2], mixed[1:amount // 2 * 2:2]
    slack = jnp.minimum(sizes[donor] - 1, most - sizes[sink]) // 2
    slack = jnp.where((donor == order[0]) | (sink == order[0]) | (sizes[sink] == 0), 0, jnp.maximum(slack, 0))
    shifted = jax.random.randint(jax.random.fold_in(own, 4), (amount // 2,), 0, 1 << 20) % (slack + 1)
    sizes = sizes.at[donor].add(-shifted).at[sink].add(shifted)
    members = jnp.searchsorted(jnp.cumsum(sizes), jnp.arange(rows * top), side="right").astype(jnp.int32)
    grid = members.reshape(top, rows).T
    grid = grid[jax.random.permutation(jax.random.fold_in(own, 1), rows)]
    offset_by = jax.random.randint(jax.random.fold_in(own, 2), (rows, 1), 0, top)
    return jnp.take_along_axis(grid, (jnp.arange(top)[None, :] + offset_by) % top, axis=1)


def shares(number_of, total, reach, skew, full):
    weights = [(1 << 20) // math.isqrt(standing ** skew) + 1 for standing in range(1, number_of + 1)]
    largest = reach if full else min(reach, max(-(-total // number_of), total * weights[0] // sum(weights)))
    least = 1 if total - largest >= number_of - 1 else 0
    holding, surplus = [largest] + [least] * (number_of - 1), total - largest - least * (number_of - 1)
    while surplus > 0:
        candidates = [i for i in range(1, number_of) if holding[i] < largest] or [i for i in range(1, number_of) if holding[i] < reach]
        mass, left = sum([weights[i] for i in candidates]), surplus
        for i in candidates:
            extra = min(reach - holding[i], max(1, left * weights[i] // mass), surplus)
            holding[i] = holding[i] + extra
            surplus = surplus - extra
    return np.array(holding)


def setup_inputs(seed: int = 0) -> dict:
    keys = jax.random.split(jax.random.key(seed), 5)
    queries = draw_queries(jax.random.fold_in(keys[4], 71), 0)
    probes_keys = jax.random.split(jax.random.fold_in(keys[1], 1), NQ // Q_DEV)
    probes_turns = jax.random.permutation(jax.random.fold_in(keys[1], 3), NQ // Q_DEV)
    probes = jax.vmap(lambda own, number: shared_out(jax.random.fold_in(keys[1], 2), own, number, Q_DEV, NPART, PROBES, CAP, 2))(probes_keys, probes_turns).reshape((NQ, PROBES))
    corpus = draw_corpus(jax.random.fold_in(keys[4], 71), 0)
    labels = place_ends(jax.random.randint(keys[3], (NPART, PROWS), 0, NCLASS), jax.random.fold_in(keys[3], 1), 0, NCLASS - 1).astype(jnp.int32)
    return dict(queries=queries, probes=probes, corpus=corpus, labels=labels)


def reference(queries, probes, corpus, labels):
    slots = DEVICES * CAP
    probe_blocks = probes.reshape(DEVICES, Q_DEV * PROBES)
    matches = (probe_blocks[:, :, None] == jnp.arange(NPART, dtype=jnp.int32)[None, None, :]).astype(jnp.int32)
    earlier = jnp.cumsum(matches, axis=1) - matches
    ranks = jnp.sum(earlier * matches, axis=-1)
    slot_ids = (jnp.arange(DEVICES, dtype=jnp.int32)[:, None] * CAP + ranks).reshape(-1).astype(jnp.int32)
    part_ids = probes.reshape(-1).astype(jnp.int32)
    query_ids = (jnp.arange(NQ * PROBES, dtype=jnp.int32) // PROBES).astype(jnp.int32)
    slot_table = jnp.full((NPART, slots), NQ, jnp.int32).at[part_ids, slot_ids].set(query_ids)
    padded = jnp.concatenate([queries, jnp.zeros((1, D), jnp.bfloat16)], axis=0)
    class_ids = jnp.arange(NCLASS, dtype=jnp.int32)

    def one_part(inputs):
        slot_rows, part_keys, part_labels = inputs
        asked_rows = padded[slot_rows]
        scores = jnp.dot(asked_rows, part_keys.T, preferred_element_type=jnp.float32) * (D ** -0.5)
        peaks = jnp.max(scores, axis=1)
        weights = jnp.exp(scores - peaks[:, None])
        stripe_tot = jnp.sum(weights.reshape(slots, N_REP, PART_ROWS_DEV), axis=2)
        totals = jnp.sum(stripe_tot, axis=1)
        shaped = weights.reshape(slots, N_REP, PART_ROWS_DEV)
        one_hot = (part_labels[:, None] == class_ids[None, :]).astype(jnp.float32).reshape(N_REP, PART_ROWS_DEV, NCLASS)
        stripe_cls = jnp.einsum("srk,rkc->src", shaped, one_hot, precision=lax.Precision.HIGHEST)
        classes = jnp.sum(stripe_cls, axis=1)
        return peaks, totals, classes

    all_peaks, all_totals, all_classes = lax.map(one_part, (slot_table, corpus, labels))
    pair_peaks = all_peaks[part_ids, slot_ids].reshape(NQ, PROBES)
    pair_totals = all_totals[part_ids, slot_ids].reshape(NQ, PROBES)
    pair_classes = all_classes[part_ids, slot_ids].reshape(NQ, PROBES, NCLASS)
    top_peak = jnp.max(pair_peaks, axis=1, keepdims=True)
    factors = jnp.exp(pair_peaks - top_peak)
    numerator = jnp.sum(factors[:, :, None] * pair_classes, axis=1)
    denominator = jnp.sum(factors * pair_totals, axis=1)
    return NCLASS * numerator / denominator[:, None]
```

```python
import functools
import math

import jax
import jax.numpy as jnp
from jax import lax
from jax.experimental import pallas as pl
from jax.experimental.pallas import tpu as pltpu
from jax.sharding import PartitionSpec as P

NCLASS = 128
CAP = 16
PARTS = 2
MESH = pl.DeviceIdType.MESH
NT = (((1,), (1,)), ((), ()))


def select_mask(probes_ref, nd):
    nq, npr = probes_ref.shape
    nparts = PARTS * nd
    width = max(128, nparts)
    part_ids = lax.broadcasted_iota(jnp.int32, (nq, width), 1)
    match = jnp.zeros((nq, width), jnp.float32)
    for j in range(npr):
        match = jnp.where(probes_ref[:, j : j + 1] == part_ids, 1.0, match)
    row = lax.broadcasted_iota(jnp.int32, (nq, nq), 0)
    col = lax.broadcasted_iota(jnp.int32, (nq, nq), 1)
    earlier = jnp.where(col < row, 1.0, 0.0).astype(jnp.bfloat16)
    rank = jnp.dot(earlier, match.astype(jnp.bfloat16), preferred_element_type=jnp.float32)
    code = jnp.where(match > 0.0, rank, -1.0)
    slots = nparts * CAP
    part_row = lax.broadcasted_iota(jnp.int32, (width, slots), 0)
    lane = lax.broadcasted_iota(jnp.int32, (width, slots), 1)
    half = nd * CAP
    lane_part = PARTS * ((lane % half) // CAP) + lane // half
    spread = jnp.where(part_row == lane_part, 1.0, 0.0).astype(jnp.bfloat16)
    wide = jnp.dot(code.astype(jnp.bfloat16), spread, preferred_element_type=jnp.float32)
    slot = (lax.broadcasted_iota(jnp.int32, (nq, slots), 1) % CAP).astype(jnp.float32)
    return jnp.where(wide == slot, 1.0, 0.0)


def kernel(
    nd, nx,
    q_ref, probes_ref, corpus_ref, labels_ref, out_ref,
    mask, outbox, inbox, kbuf, lab, acc, m_s, mout, pin, ret,
    ks, kr, qs, qr, ls, lr, rs, rr, ps, pr,
):
    dom = lax.axis_index("dom")
    rep = lax.axis_index("rep")
    nrep = 2 * nx
    x, c = rep // 2, rep % 2
    rows = corpus_ref.shape[1]
    hr = rows // 2
    half = nd * CAP
    right = (dom, ((x + 1) % nx) * 2 + c)
    left = (dom, ((x + nx - 1) % nx) * 2 + c)
    sibling = (dom, x * 2 + (1 - c))

    barrier = pltpu.get_barrier_semaphore()

    def greet_dom(k, carry):
        pl.semaphore_signal(barrier, inc=1, device_id=((dom + k) % nd, rep), device_id_type=MESH)
        return carry

    def greet_rep(k, carry):
        pl.semaphore_signal(barrier, inc=1, device_id=(dom, (rep + k) % nrep), device_id_type=MESH)
        return carry

    lax.fori_loop(1, nd, greet_dom, 0)
    lax.fori_loop(1, nrep, greet_rep, 0)

    def own_copy(p, h):
        return pltpu.make_async_copy(
            corpus_ref.at[p, pl.ds(h * hr, hr)], kbuf.at[p, rep, pl.ds(h * hr, hr)], kr.at[p, rep, h]
        )

    for p in range(PARTS):
        for h in range(2):
            own_copy(p, h).start()
    own_lab = pltpu.make_async_copy(labels_ref, lab.at[rep], lr)
    own_lab.start()

    sel = select_mask(probes_ref, nd)
    mask[...] = sel
    picked = lax.dot_general(
        sel.T.astype(jnp.bfloat16), q_ref[...], (((1,), (0,)), ((), ())), preferred_element_type=jnp.float32
    )
    outbox[...] = picked.astype(jnp.bfloat16).reshape(outbox.shape)

    pl.semaphore_wait(barrier, nd - 1 + nrep - 1)

    def send(p, chunk, h, device, k):
        rows_h = pl.ds(h * hr, hr)
        return pltpu.make_async_remote_copy(
            src_ref=kbuf.at[p, chunk, rows_h],
            dst_ref=kbuf.at[p, chunk, rows_h],
            send_sem=ks.at[p, k],
            recv_sem=kr.at[p, chunk, h],
            device_id=device,
            device_id_type=MESH,
        )

    def chunk_at(dx, col):
        return ((x + dx) % nx) * 2 + col

    cl, cr, co = chunk_at(nx - 1, c), chunk_at(1, c), chunk_at(2, c)

    def moves(p):
        return {
            "r0": (p, rep, 0, right, 0),
            "r1": (p, rep, 1, right, 1),
            "l1": (p, rep, 1, left, 2),
            "l0": (p, rep, 0, left, 3),
            "rr": (p, cl, 0, right, 4),
            "ll": (p, cr, 1, left, 5),
            "s0": (p, rep, 0, sibling, 6),
            "s1": (p, rep, 1, sibling, 7),
            "sl0": (p, cl, 0, sibling, 8),
            "sl1": (p, cl, 1, sibling, 9),
            "sr0": (p, cr, 0, sibling, 10),
            "sr1": (p, cr, 1, sibling, 11),
            "so0": (p, co, 0, sibling, 12),
            "so1": (p, co, 1, sibling, 13),
        }

    def start(p, *names):
        table = moves(p)
        for name in names:
            send(*table[name]).start()

    def arrive(p, chunk, h):
        piece = kbuf.at[p, chunk, pl.ds(h * hr, hr)]
        pltpu.make_async_copy(piece, piece, kr.at[p, chunk, h]).wait()

    arrive(0, rep, 0)
    arrive(0, rep, 1)
    start(0, "r0", "l1", "s0", "s1")

    def send_query(k, carry):
        peer = (dom + k) % nd
        pltpu.make_async_remote_copy(
            src_ref=outbox.at[:, peer],
            dst_ref=inbox.at[:, dom],
            send_sem=qs,
            recv_sem=qr,
            device_id=(peer, rep),
            device_id_type=MESH,
        ).start()
        return carry

    pltpu.make_async_copy(outbox.at[:, dom], inbox.at[:, dom], qr).start()
    lax.fori_loop(1, nd, send_query, 0)
    start(0, "r1", "l0")

    def send_label(k, carry):
        pltpu.make_async_remote_copy(
            src_ref=labels_ref,
            dst_ref=lab.at[rep],
            send_sem=ls,
            recv_sem=lr,
            device_id=(dom, (rep + k) % nrep),
            device_id_type=MESH,
        ).start()
        return carry

    lax.fori_loop(1, nrep, send_label, 0)
    arrive(1, rep, 0)
    arrive(1, rep, 1)
    start(1, "s0", "s1")

    log2e = math.log2(math.e) * (q_ref.shape[1] ** -0.5)

    def unit(p, chunk, h):
        keys = kbuf[p, chunk, pl.ds(h * hr, hr), :]
        named = lab[chunk, p : p + 1, pl.ds(pl.multiple_of(h * hr, hr), hr)]
        onehot = jnp.where(
            lax.broadcasted_iota(jnp.int32, (NCLASS, hr), 0) == named, 1.0, 0.0
        ).astype(jnp.bfloat16)
        bs = min(half, 256)
        for b in range(half // bs):
            at = pl.ds(b * bs, bs)
            doms = pl.ds(b * bs // CAP, bs // CAP)
            queries = inbox[p, doms].reshape(bs, -1)
            scores = lax.dot_general(queries, keys, NT, preferred_element_type=jnp.float32)
            m_old = m_s[at, :]
            m_new = jnp.maximum(m_old, jnp.max(scores, axis=1, keepdims=True))
            m_s[at, :] = m_new
            fade = jnp.exp2((m_old - m_new) * log2e)
            weights = jnp.exp2((scores - m_new[:, :1]) * log2e)
            high = weights.astype(jnp.bfloat16)
            low = (weights - high.astype(jnp.float32)).astype(jnp.bfloat16)
            sums = lax.dot_general(high, onehot, NT, preferred_element_type=jnp.float32)
            sums += lax.dot_general(low, onehot, NT, preferred_element_type=jnp.float32)
            old = acc[p, doms].reshape(bs, NCLASS)
            acc[p, doms] = (old * fade + sums).reshape(bs // CAP, CAP, NCLASS)

    def loop4(fn):
        def body(j, carry):
            fn(j)
            return carry

        lax.fori_loop(0, 4, body, 0)

    def own_units(p, ready):
        def fn(j):
            chunk = x * 2 + (c + j // 2) % 2
            if ready:
                pl.when(j >= 2)(lambda: arrive(p, chunk, j % 2))
            unit(p, chunk, j % 2)

        loop4(fn)

    def near_units(p, col, wait):
        def fn(j):
            chunk = ((x + nx - 1 + 2 * (j % 2)) % nx) * 2 + col
            h = ((j + 1) // 2) % 2
            if wait:
                arrive(p, chunk, h)
            unit(p, chunk, h)

        loop4(fn)

    def far_units(p):
        def fn(j):
            chunk = ((x + 2) % nx) * 2 + (c + j // 2) % 2
            pl.when(j >= 2)(lambda: arrive(p, chunk, j % 2))
            unit(p, chunk, j % 2)

        loop4(fn)

    def first_near(p):
        arrive(p, cl, 0)
        start(p, "rr", "sl0")
        arrive(p, cr, 1)
        start(p, "ll", "sr1")

    def second_near(p):
        arrive(p, cl, 1)
        arrive(p, cr, 0)
        start(p, "sl1", "sr0")

    def far(p):
        arrive(p, co, 0)
        start(p, "so0")
        arrive(p, co, 1)
        start(p, "so1")

    def reset(p):
        m_s[...] = jnp.full(m_s.shape, -3.0e38, jnp.float32)
        acc[p] = jnp.zeros(acc.shape[1:], jnp.float32)

    def send_back(p):
        def one(k, carry):
            peer = (dom + k) % nd
            pltpu.make_async_remote_copy(
                src_ref=acc.at[p, peer],
                dst_ref=ret.at[p, dom],
                send_sem=rs.at[p],
                recv_sem=rr.at[p],
                device_id=(peer, rep),
                device_id_type=MESH,
            ).start()
            return carry

        pltpu.make_async_copy(acc.at[p, dom], ret.at[p, dom], rr.at[p]).start()
        lax.fori_loop(1, nd, one, 0)
        lane = lax.broadcasted_iota(jnp.int32, (half, 128), 1) % CAP
        slot = lax.broadcasted_iota(jnp.int32, (half, 128), 0) % CAP
        diag = jnp.where(lane == slot, m_s[...], 0.0).reshape(nd, CAP, 128)
        mout[p] = jnp.sum(diag, axis=1, keepdims=True)

    def send_peaks():
        def one(k, carry):
            peer = (dom + k) % nd
            pltpu.make_async_remote_copy(
                src_ref=mout.at[:, peer],
                dst_ref=pin.at[:, dom],
                send_sem=ps,
                recv_sem=pr,
                device_id=(peer, rep),
                device_id_type=MESH,
            ).start()
            return carry

        pltpu.make_async_copy(mout.at[:, dom], pin.at[:, dom], pr).start()
        lax.fori_loop(1, nd, one, 0)

    first_near(0)
    second_near(0)
    start(1, "r0", "l1", "r1", "l0")
    reset(0)
    pltpu.make_async_copy(lab, lab, lr).wait()
    pltpu.make_async_copy(inbox, inbox, qr).wait()
    own_units(0, True)
    near_units(0, c, False)
    far(0)
    near_units(0, 1 - c, True)
    far_units(0)
    send_back(0)
    first_near(1)
    reset(1)
    own_units(1, True)
    second_near(1)
    near_units(1, c, False)
    near_units(1, 1 - c, True)
    far(1)
    far_units(1)
    send_back(1)
    send_peaks()

    for p in range(PARTS):
        for move in moves(p).values():
            send(*move).wait_send()
    others = pl.ds(0, nd - 1)
    pltpu.make_async_copy(outbox.at[:, others], outbox.at[:, others], qs).wait()
    few = pl.ds(0, nrep - 1)
    pltpu.make_async_copy(lab.at[few], lab.at[few], ls).wait()
    for p in range(PARTS):
        pltpu.make_async_copy(acc.at[p, others], acc.at[p, others], rs.at[p]).wait()
    pltpu.make_async_copy(mout.at[:, others], mout.at[:, others], ps).wait()

    pltpu.make_async_copy(pin, pin, pr).wait()
    pltpu.make_async_copy(ret.at[0], ret.at[0], rr.at[0]).wait()
    pltpu.make_async_copy(ret.at[1], ret.at[1], rr.at[1]).wait()
    nq = q_ref.shape[0]
    per = 128 // CAP
    gl = min(128, half)
    lane = lax.broadcasted_iota(jnp.int32, (1, 128), 1) // CAP
    peak_rows = []
    top = jnp.full((nq, 1), -3.0e38, jnp.float32)
    groups = [(p, g) for p in range(PARTS) for g in range(half // 128)]
    for p, g in groups:
        line = jnp.zeros((1, 128), jnp.float32)
        for i in range(per):
            line = jnp.where(lane == i, pin[p, g * per + i], line)
        peak_rows.append(line)
        chosen = mask[:, p * half + g * 128 : p * half + (g + 1) * 128] > 0.0
        top = jnp.maximum(top, jnp.max(jnp.where(chosen, line, -3.0e38), axis=1, keepdims=True))
    total = jnp.zeros((nq, NCLASS), jnp.float32)
    for (p, g), line in zip(groups, peak_rows):
        chosen = mask[:, p * half + g * 128 : p * half + (g + 1) * 128] > 0.0
        factor = jnp.where(chosen, jnp.exp2(jnp.where(chosen, line - top, 0.0) * log2e), 0.0)
        block = ret[p, g * per : (g + 1) * per].reshape(128, NCLASS)
        total += jnp.dot(factor, block, precision=lax.Precision.HIGHEST, preferred_element_type=jnp.float32)
    out_ref[...] = NCLASS * total / jnp.sum(total, axis=1, keepdims=True)


def local(queries, probes, corpus, labels):
    nd = lax.axis_size("dom")
    nrep = lax.axis_size("rep")
    nq, depth = queries.shape
    rows = corpus.shape[1]
    half = nd * CAP
    vmem = pl.BlockSpec(memory_space=pltpu.VMEM)
    dma = pltpu.SemaphoreType.DMA
    return pl.pallas_call(
        functools.partial(kernel, nd, nrep // 2),
        out_shape=jax.ShapeDtypeStruct((nq, NCLASS), jnp.float32),
        in_specs=[vmem, vmem, pl.BlockSpec(memory_space=pl.ANY), vmem],
        out_specs=vmem,
        scratch_shapes=[
            pltpu.VMEM((nq, PARTS * half), jnp.float32),
            pltpu.VMEM((PARTS, nd, CAP, depth), jnp.bfloat16),
            pltpu.VMEM((PARTS, nd, CAP, depth), jnp.bfloat16),
            pltpu.VMEM((PARTS, nrep, rows, depth), jnp.bfloat16),
            pltpu.VMEM((nrep, PARTS, rows), jnp.int32),
            pltpu.VMEM((PARTS, nd, CAP, NCLASS), jnp.float32),
            pltpu.VMEM((half, 128), jnp.float32),
            pltpu.VMEM((PARTS, nd, 1, 128), jnp.float32),
            pltpu.VMEM((PARTS, nd, 1, 128), jnp.float32),
            pltpu.VMEM((PARTS, nd, CAP, NCLASS), jnp.float32),
            dma((PARTS, 14)),
            dma((PARTS, nrep, 2)),
            dma, dma, dma, dma,
            dma((PARTS,)),
            dma((PARTS,)),
            dma, dma,
        ],
        compiler_params=pltpu.CompilerParams(
            collective_id=0, has_side_effects=True, vmem_limit_bytes=48 * 1024 * 1024
        ),
    )(queries, probes, corpus, labels)


def solution(mesh):
    in_specs = (
        P(("dom", "rep"), None),
        P(("dom", "rep"), None),
        P("dom", "rep", None),
        P("dom", "rep"),
    )
    out_specs = P(("dom", "rep"), None)
    return jax.shard_map(local, mesh=mesh, in_specs=in_specs, out_specs=out_specs, check_vma=False)
```

```python
import functools
import math

import jax
import jax.numpy as jnp
from jax import lax
from jax.experimental import pallas as pl
from jax.experimental.pallas import tpu as pltpu
from jax.sharding import PartitionSpec as P

NCLASS = 128
CAP = 16
PARTS = 2
WINDOW = 4
STEPS = 32767.0
MESH = pl.DeviceIdType.MESH
NT = (((1,), (1,)), ((), ()))


def select_slots(named, nd):
    npr, nq = named.shape
    nparts = PARTS * nd
    width = max(128, nparts)
    part_ids = lax.broadcasted_iota(jnp.int32, (width, nq), 0)
    match = jnp.zeros((width, nq), jnp.float32)
    for j in range(npr):
        match = jnp.where(named[j : j + 1, :] == part_ids, 1.0, match)
    row = lax.broadcasted_iota(jnp.int32, (nq, nq), 0)
    col = lax.broadcasted_iota(jnp.int32, (nq, nq), 1)
    earlier = jnp.where(row < col, 1.0, 0.0).astype(jnp.bfloat16)
    rank = jnp.dot(match.astype(jnp.bfloat16), earlier, preferred_element_type=jnp.float32)
    code = jnp.where(match > 0.0, rank, -1.0)
    slots = nparts * CAP
    half = nd * CAP
    slot_row = lax.broadcasted_iota(jnp.int32, (slots, width), 0)
    slot_part = PARTS * ((slot_row % half) // CAP) + slot_row // half
    spread = jnp.where(lax.broadcasted_iota(jnp.int32, (slots, width), 1) == slot_part, 1.0, 0.0)
    wide = jnp.dot(
        spread.astype(jnp.bfloat16), code.astype(jnp.bfloat16), preferred_element_type=jnp.float32
    )
    slot = (lax.broadcasted_iota(jnp.int32, (slots, nq), 0) % CAP).astype(jnp.float32)
    return jnp.where(wide == slot, 1.0, 0.0)


def kernel(
    nd, nx,
    q_hbm, probes_hbm, corpus_hbm, labels_hbm, out_ref,
    q_ref, probes_ref, mask, outbox, inbox, kbuf, lab, acc, m_s, wire, mout, pin, ret,
    fs, ko, so_s, so_r, ks, kr, bs_s, bs_r, qs, qr, ls, lr, rs, rr, ps, pr,
):
    dom = lax.axis_index("dom")
    rep = lax.axis_index("rep")
    nrep = 2 * nx
    x, c = rep // 2, rep % 2
    rows = kbuf.shape[2]
    qrows = rows // 4
    half = nd * CAP
    nz = min(nd, 8)
    ny = nd // nz
    y, z = dom // nz, dom % nz
    right = (dom, ((x + 1) % nx) * 2 + c)
    left = (dom, ((x + nx - 1) % nx) * 2 + c)
    sibling = (dom, x * 2 + (1 - c))

    barrier = pltpu.get_barrier_semaphore()

    def greet_dom(k, carry):
        pl.semaphore_signal(barrier, inc=1, device_id=((dom + k) % nd, rep), device_id_type=MESH)
        return carry

    def greet_rep(k, carry):
        pl.semaphore_signal(barrier, inc=1, device_id=(dom, (rep + k) % nrep), device_id_type=MESH)
        return carry

    lax.fori_loop(1, nrep, greet_rep, 0)
    lax.fori_loop(1, nd, greet_dom, 0)

    get_probes = pltpu.make_async_copy(probes_hbm, probes_ref, fs.at[0])
    get_queries = pltpu.make_async_copy(q_hbm, q_ref, fs.at[1])
    get_labels = pltpu.make_async_copy(labels_hbm, lab.at[rep], fs.at[2])
    get_rows = [
        pltpu.make_async_copy(corpus_hbm.at[p], kbuf.at[p, rep], ko.at[p]) for p in range(PARTS)
    ]
    for copy in (get_probes, get_queries, get_rows[0], get_labels, get_rows[1]):
        copy.start()
    get_rows[0].wait()

    pl.semaphore_wait(barrier, nd - 1 + nrep - 1)

    def piece(p, xx, col, quarter):
        return kbuf.at[p, xx * 2 + col, pl.ds(pl.multiple_of(quarter * qrows, qrows), qrows)]

    def ring(way, g):
        p, k = g // 6, g % 6
        if way == 0:
            ref = piece(p, (x + nx - k // 4) % nx, c, k % 4)
        else:
            ref = piece(p, (x + k // 4) % nx, c, 3 - k % 4)
        return pltpu.make_async_remote_copy(
            src_ref=ref, dst_ref=ref, send_sem=ks.at[way, g], recv_sem=kr.at[way, g],
            device_id=right if way == 0 else left, device_id_type=MESH,
        )

    def landed(way, g, col):
        p, k = g // 6, g % 6
        if way == 0:
            return p, (x + 2 * nx - 1 - k // 4) % nx, col, k % 4
        return p, (x + 1 + k // 4) % nx, col, 3 - k % 4

    def share(way, g):
        ref = piece(*landed(way, g, c))
        return pltpu.make_async_remote_copy(
            src_ref=ref, dst_ref=ref, send_sem=bs_s.at[way, g], recv_sem=bs_r.at[way, g],
            device_id=sibling, device_id_type=MESH,
        )

    def share_own(p):
        ref = kbuf.at[p, rep]
        return pltpu.make_async_remote_copy(
            src_ref=ref, dst_ref=ref, send_sem=so_s.at[p], recv_sem=so_r.at[p],
            device_id=sibling, device_id_type=MESH,
        )

    for g in range(WINDOW):
        ring(0, g).start()
        ring(1, g).start()

    get_probes.wait()
    get_queries.wait()
    sel = select_slots(probes_ref[...], nd)
    picked = jnp.dot(sel.astype(jnp.bfloat16), q_ref[...], preferred_element_type=jnp.float32)
    outbox[...] = picked.astype(jnp.bfloat16).reshape(outbox.shape)
    get_labels.wait()
    get_rows[1].wait()


    def peer_of(t):
        i, j = t // ny, t % ny
        dz = nz // 2 + (1 - 2 * (i % 2)) * ((i + 1) // 2)
        dy = ny // 2 + (1 - 2 * (j % 2)) * ((j + 1) // 2)
        return ((y + dy) % ny) * nz + (z + dz) % nz

    def to_all(src, dst, send_sem, recv_sem):
        def one(t, carry):
            peer = peer_of(t)
            pltpu.make_async_remote_copy(
                src_ref=src(peer), dst_ref=dst(dom), send_sem=send_sem, recv_sem=recv_sem,
                device_id=(peer, rep), device_id_type=MESH,
            ).start()
            return carry

        lax.fori_loop(0, nd - 1, one, 0)
        pltpu.make_async_copy(src(dom), dst(dom), recv_sem).start()

    to_all(lambda d: outbox.at[:, d], lambda d: inbox.at[:, d], qs, qr)

    def send_label(k, carry):
        pltpu.make_async_remote_copy(
            src_ref=lab.at[rep], dst_ref=lab.at[rep], send_sem=ls, recv_sem=lr,
            device_id=(dom, (rep + k) % nrep), device_id_type=MESH,
        ).start()
        return carry

    lax.fori_loop(1, nrep, send_label, 0)
    share_own(0).start()

    def event(g):
        for way in range(2):
            ref = piece(*landed(way, g, c))
            pltpu.make_async_copy(ref, ref, kr.at[way, g]).wait()
            share(way, g).start()

        @pl.when(g + WINDOW < 12)
        def _():
            ring(0, g + WINDOW).start()
            ring(1, g + WINDOW).start()

    log2e = math.log2(math.e) * (q_ref.shape[1] ** -0.5)

    def unit(p, pieces):
        queries = inbox[p].reshape(half, -1)
        scores, onehots = [], []
        for _, xx, col, quarter in pieces:
            at = pl.ds(pl.multiple_of(quarter * qrows, qrows), qrows)
            keys = kbuf[p, xx * 2 + col, at, :]
            named = lab[xx * 2 + col, p : p + 1, at]
            classes = lax.broadcasted_iota(jnp.int32, (NCLASS, qrows), 0)
            onehots.append(jnp.where(classes == named, 1.0, 0.0).astype(jnp.bfloat16))
            scores.append(lax.dot_general(queries, keys, NT, preferred_element_type=jnp.float32))
        scores = jnp.concatenate(scores, axis=1)
        m_old = m_s[...]
        m_new = jnp.maximum(m_old, jnp.max(scores, axis=1, keepdims=True))
        m_s[...] = m_new
        fade = jnp.exp2((m_old - m_new) * log2e)
        wide = jnp.concatenate([m_new] * (scores.shape[1] // 128), axis=1)
        weights = jnp.exp2((scores - wide) * log2e)
        high = weights.astype(jnp.bfloat16)
        low = (weights - high.astype(jnp.float32)).astype(jnp.bfloat16)
        sums = lax.dot_general(
            jnp.concatenate([high, low], axis=1), jnp.concatenate(onehots * 2, axis=1), NT,
            preferred_element_type=jnp.float32,
        )
        acc[...] = acc[...] * fade + sums

    def own_units(p):
        m_s[...] = jnp.full(m_s.shape, -3.0e38, jnp.float32)
        acc[...] = jnp.zeros(acc.shape, jnp.float32)

        def body(i, carry):
            col = (c + i) % 2

            @pl.when(i == 1)
            def _():
                ref = kbuf.at[p, x * 2 + col]
                pltpu.make_async_copy(ref, ref, so_r.at[p]).wait()

            unit(p, [(p, x, col, quarter) for quarter in range(4)])
            return carry

        lax.fori_loop(0, 2, body, 0)

    def here(g):
        return [landed(way, g, c) for way in range(2)]

    def there(g):
        pieces = [landed(way, g, 1 - c) for way in range(2)]
        for way in range(2):
            ref = piece(*pieces[way])
            pltpu.make_async_copy(ref, ref, bs_r.at[way, g]).wait()
        return pieces

    def finish(p):
        lane = lax.broadcasted_iota(jnp.int32, (half, 128), 1) % CAP
        slot = lax.broadcasted_iota(jnp.int32, (half, 128), 0) % CAP
        diag = jnp.where(lane == slot, m_s[...], 0.0).reshape(nd, CAP, 128)
        mout[p, :, 0] = jnp.sum(diag, axis=1, keepdims=True)
        sums = acc[...]
        most = jnp.max(sums, axis=1, keepdims=True)
        diag = jnp.where(lane == slot, most, 0.0).reshape(nd, CAP, 128)
        mout[p, :, 1] = jnp.sum(diag, axis=1, keepdims=True)
        codes = jnp.round(sums * (STEPS / most)).astype(jnp.int32).astype(jnp.int16)
        wire[p] = codes.reshape(nd, CAP, NCLASS)

    def send_back(p):
        to_all(lambda d: wire.at[p, d], lambda d: ret.at[p, d], rs.at[p], rr.at[p])
        to_all(lambda d: mout.at[p, d], lambda d: pin.at[p, d], ps.at[p], pr.at[p])

    event(0)
    event(1)
    mask[...] = sel.T
    pltpu.make_async_copy(lab.at[pl.ds(0, nrep - 1)], lab.at[pl.ds(0, nrep - 1)], lr).wait()
    pltpu.make_async_copy(inbox, inbox, qr).wait()
    own_units(0)
    share_own(1).start()

    def first(g, carry):
        event(g + 2)
        unit(0, here(g) + there(g))
        return carry

    lax.fori_loop(0, 6, first, 0)
    finish(0)
    send_back(0)
    own_units(1)

    def second(g, carry):
        pl.when(g > 6)(lambda: event(g + 1))
        unit(1, here(g) + there(g))
        return carry

    lax.fori_loop(6, 11, second, 0)
    unit(1, here(11))
    unit(1, there(11))
    finish(1)
    send_back(1)

    def gone(g, carry):
        for way in range(2):
            ring(way, g).wait_send()
            share(way, g).wait_send()
        return carry

    lax.fori_loop(0, 12, gone, 0)
    for p in range(PARTS):
        share_own(p).wait_send()
    others = pl.ds(0, nd - 1)
    few = pl.ds(0, nrep - 1)
    pltpu.make_async_copy(outbox.at[:, others], outbox.at[:, others], qs).wait()
    pltpu.make_async_copy(lab.at[few], lab.at[few], ls).wait()

    def left_home(p):
        pltpu.make_async_copy(wire.at[p, others], wire.at[p, others], rs.at[p]).wait()
        pltpu.make_async_copy(mout.at[p, others], mout.at[p, others], ps.at[p]).wait()

    left_home(0)

    nq = q_ref.shape[0]
    per = 128 // CAP
    lane = lax.broadcasted_iota(jnp.int32, (1, 128), 1) // CAP
    top = jnp.full((nq, 1), -3.0e38, jnp.float32)
    total = jnp.zeros((nq, NCLASS), jnp.float32)
    for p in range(PARTS):
        pltpu.make_async_copy(pin.at[p], pin.at[p], pr.at[p]).wait()
        found = []
        new_top = top
        for g in range(half // 128):
            line = jnp.zeros((1, 128), jnp.float32)
            most = jnp.zeros((1, 128), jnp.float32)
            for i in range(per):
                line = jnp.where(lane == i, pin[p, g * per + i, 0], line)
                most = jnp.where(lane == i, pin[p, g * per + i, 1], most)
            chosen = mask[:, p * half + g * 128 : p * half + (g + 1) * 128] > 0.0
            found.append((chosen, line, most))
            best = jnp.max(jnp.where(chosen, line, -3.0e38), axis=1, keepdims=True)
            new_top = jnp.maximum(new_top, best)
        total = total * jnp.exp2((top - new_top) * log2e)
        top = new_top
        factors = [
            jnp.where(chosen, jnp.exp2(jnp.where(chosen, line - top, 0.0) * log2e) * (most / STEPS), 0.0)
            for chosen, line, most in found
        ]
        pltpu.make_async_copy(ret.at[p], ret.at[p], rr.at[p]).wait()
        for g, factor in enumerate(factors):
            block = ret[p, g * per : (g + 1) * per].astype(jnp.int32).astype(jnp.float32).reshape(128, NCLASS)
            total += jnp.dot(factor, block, precision=lax.Precision.HIGHEST, preferred_element_type=jnp.float32)
    out_ref[...] = NCLASS * total / jnp.sum(total, axis=1, keepdims=True)
    left_home(1)


def local(queries, probes, corpus, labels):
    nd = lax.axis_size("dom")
    nrep = lax.axis_size("rep")
    nq, depth = queries.shape
    rows = corpus.shape[1]
    half = nd * CAP
    dma = pltpu.SemaphoreType.DMA
    return pl.pallas_call(
        functools.partial(kernel, nd, nrep // 2),
        out_shape=jax.ShapeDtypeStruct((nq, NCLASS), jnp.float32),
        in_specs=[pl.BlockSpec(memory_space=pl.ANY)] * 4,
        out_specs=pl.BlockSpec(memory_space=pltpu.VMEM),
        scratch_shapes=[
            pltpu.VMEM((nq, depth), jnp.bfloat16),
            pltpu.VMEM((probes.shape[1], nq), jnp.int32),
            pltpu.VMEM((nq, PARTS * half), jnp.float32),
            pltpu.VMEM((PARTS, nd, CAP, depth), jnp.bfloat16),
            pltpu.VMEM((PARTS, nd, CAP, depth), jnp.bfloat16),
            pltpu.VMEM((PARTS, nrep, rows, depth), jnp.bfloat16),
            pltpu.VMEM((nrep, PARTS, rows), jnp.int32),
            pltpu.VMEM((half, NCLASS), jnp.float32),
            pltpu.VMEM((half, 128), jnp.float32),
            pltpu.VMEM((PARTS, nd, CAP, NCLASS), jnp.int16),
            pltpu.VMEM((PARTS, nd, 2, 1, 128), jnp.float32),
            pltpu.VMEM((PARTS, nd, 2, 1, 128), jnp.float32),
            pltpu.VMEM((PARTS, nd, CAP, NCLASS), jnp.int16),
            dma((3,)),
            dma((PARTS,)),
            dma((PARTS,)),
            dma((PARTS,)),
            dma((2, 12)),
            dma((2, 12)),
            dma((2, 12)),
            dma((2, 12)),
            dma, dma, dma, dma,
            dma((PARTS,)),
            dma((PARTS,)),
            dma((PARTS,)),
            dma((PARTS,)),
        ],
        compiler_params=pltpu.CompilerParams(
            collective_id=0, has_side_effects=True, vmem_limit_bytes=62 * 1024 * 1024
        ),
    )(queries, probes.T, corpus, labels)


def solution(mesh):
    in_specs = (
        P(("dom", "rep"), None),
        P(("dom", "rep"), None),
        P("dom", "rep", None),
        P("dom", "rep"),
    )
    out_specs = P(("dom", "rep"), None)
    return jax.shard_map(local, mesh=mesh, in_specs=in_specs, out_specs=out_specs, check_vma=False)
```

```python
import functools
import math

import jax
import jax.numpy as jnp
from jax import lax
from jax.experimental import pallas as pl
from jax.experimental.pallas import tpu as pltpu
from jax.sharding import PartitionSpec as P

NCLASS = 128
CAP = 16
PARTS = 2
WINDOW = 4
STEPS = 32767.0
MESH = pl.DeviceIdType.MESH
NT = (((1,), (1,)), ((), ()))


def select_slots(named, nd):
    npr, nq = named.shape
    nparts = PARTS * nd
    width = max(128, nparts)
    part_ids = lax.broadcasted_iota(jnp.int32, (width, nq), 0)
    match = jnp.zeros((width, nq), jnp.float32)
    for j in range(npr):
        match = jnp.where(named[j : j + 1, :] == part_ids, 1.0, match)
    row = lax.broadcasted_iota(jnp.int32, (nq, nq), 0)
    col = lax.broadcasted_iota(jnp.int32, (nq, nq), 1)
    earlier = jnp.where(row < col, 1.0, 0.0).astype(jnp.bfloat16)
    rank = jnp.dot(match.astype(jnp.bfloat16), earlier, preferred_element_type=jnp.float32)
    code = jnp.where(match > 0.0, rank, -1.0)
    slots = nparts * CAP
    half = nd * CAP
    slot_row = lax.broadcasted_iota(jnp.int32, (slots, width), 0)
    slot_part = PARTS * ((slot_row % half) // CAP) + slot_row // half
    spread = jnp.where(lax.broadcasted_iota(jnp.int32, (slots, width), 1) == slot_part, 1.0, 0.0)
    wide = jnp.dot(
        spread.astype(jnp.bfloat16), code.astype(jnp.bfloat16), preferred_element_type=jnp.float32
    )
    slot = (lax.broadcasted_iota(jnp.int32, (slots, nq), 0) % CAP).astype(jnp.float32)
    return jnp.where(wide == slot, 1.0, 0.0)


def kernel(
    nd, nx,
    q_hbm, probes_hbm, corpus_hbm, labels_hbm, out_ref,
    q_ref, probes_ref, mask, outbox, inbox, kbuf, lab, acc, m_s, wire, mout, pin, ret,
    fs, ko, so_s, so_r, ks, kr, bs_s, bs_r, qs, qr, ls, lr, rs, rr, ps, pr,
):
    dom = lax.axis_index("dom")
    rep = lax.axis_index("rep")
    nrep = 2 * nx
    x, c = lax.div(rep, 2), lax.rem(rep, 2)
    rows = kbuf.shape[2]
    qrows = rows // 4
    half = nd * CAP
    nz = min(nd, 8)
    ny = nd // nz
    y, z = lax.div(dom, nz), lax.rem(dom, nz)
    right = (dom, lax.rem(x + 1, nx) * 2 + c)
    left = (dom, lax.rem(x + nx - 1, nx) * 2 + c)
    sibling = (dom, x * 2 + (1 - c))

    lines = [
        lax.rem(y + (ny // 2 + (1 - 2 * (j % 2)) * ((j + 1) // 2)), ny) * nz for j in range(ny)
    ]

    def each_peer(act):
        def one(i, carry):
            dz = nz // 2 + (1 - 2 * lax.rem(i, 2)) * lax.div(i + 1, 2)
            there = lax.rem(z + dz, nz)
            for line in lines:
                act(line + there)
            return carry

        lax.fori_loop(0, nz - 1, one, 0)
        for line in lines[:-1]:
            act(line + z)

    barrier = pltpu.get_barrier_semaphore()

    def greet(device):
        pl.semaphore_signal(barrier, inc=1, device_id=device, device_id_type=MESH)

    each_peer(lambda peer: greet((peer, rep)))
    for k in range(1, nrep):
        greet((dom, lax.rem(rep + k, nrep)))

    get_probes = pltpu.make_async_copy(probes_hbm, probes_ref, fs.at[0])
    get_queries = pltpu.make_async_copy(q_hbm, q_ref, fs.at[1])
    get_labels = pltpu.make_async_copy(labels_hbm, lab.at[rep], fs.at[2])
    get_rows = [
        pltpu.make_async_copy(corpus_hbm.at[p], kbuf.at[p, rep], ko.at[p]) for p in range(PARTS)
    ]
    for copy in (get_probes, get_queries, get_rows[0], get_labels, get_rows[1]):
        copy.start()
    get_rows[0].wait()

    pl.semaphore_wait(barrier, nd - 1 + nrep - 1)

    def piece(p, xx, col, quarter):
        return kbuf.at[p, xx * 2 + col, pl.ds(pl.multiple_of(quarter * qrows, qrows), qrows)]

    def ring(way, g):
        p, k = lax.div(g, 6), lax.rem(g, 6)
        if way == 0:
            ref = piece(p, lax.rem(x + nx - lax.div(k, 4), nx), c, lax.rem(k, 4))
        else:
            ref = piece(p, lax.rem(x + lax.div(k, 4), nx), c, 3 - lax.rem(k, 4))
        return pltpu.make_async_remote_copy(
            src_ref=ref, dst_ref=ref, send_sem=ks.at[way, g], recv_sem=kr.at[way, g],
            device_id=right if way == 0 else left, device_id_type=MESH,
        )

    def landed(way, g, col):
        p, k = lax.div(g, 6), lax.rem(g, 6)
        if way == 0:
            return p, lax.rem(x + 2 * nx - 1 - lax.div(k, 4), nx), col, lax.rem(k, 4)
        return p, lax.rem(x + 1 + lax.div(k, 4), nx), col, 3 - lax.rem(k, 4)

    def share(way, g):
        ref = piece(*landed(way, g, c))
        return pltpu.make_async_remote_copy(
            src_ref=ref, dst_ref=ref, send_sem=bs_s.at[way, g], recv_sem=bs_r.at[way, g],
            device_id=sibling, device_id_type=MESH,
        )

    def share_own(p):
        ref = kbuf.at[p, rep]
        return pltpu.make_async_remote_copy(
            src_ref=ref, dst_ref=ref, send_sem=so_s.at[p], recv_sem=so_r.at[p],
            device_id=sibling, device_id_type=MESH,
        )

    for g in range(WINDOW):
        ring(0, g).start()
        ring(1, g).start()

    get_probes.wait()
    get_queries.wait()
    sel = select_slots(probes_ref[...], nd)
    picked = jnp.dot(sel.astype(jnp.bfloat16), q_ref[...], preferred_element_type=jnp.float32)
    outbox[...] = picked.astype(jnp.bfloat16).reshape(outbox.shape)
    get_labels.wait()
    get_rows[1].wait()


    def to_all(src, dst, send_sem, recv_sem):
        def send(peer):
            pltpu.make_async_remote_copy(
                src_ref=src(peer), dst_ref=dst(dom), send_sem=send_sem, recv_sem=recv_sem,
                device_id=(peer, rep), device_id_type=MESH,
            ).start()

        each_peer(send)
        pltpu.make_async_copy(src(dom), dst(dom), recv_sem).start()

    to_all(lambda d: outbox.at[:, d], lambda d: inbox.at[:, d], qs, qr)

    for k in range(1, nrep):
        pltpu.make_async_remote_copy(
            src_ref=lab.at[rep], dst_ref=lab.at[rep], send_sem=ls, recv_sem=lr,
            device_id=(dom, lax.rem(rep + k, nrep)), device_id_type=MESH,
        ).start()
    share_own(0).start()

    def event(g):
        for way in range(2):
            ref = piece(*landed(way, g, c))
            pltpu.make_async_copy(ref, ref, kr.at[way, g]).wait()
            share(way, g).start()

        @pl.when(g + WINDOW < 12)
        def _():
            ring(0, g + WINDOW).start()
            ring(1, g + WINDOW).start()

    log2e = math.log2(math.e) * (q_ref.shape[1] ** -0.5)

    def unit(p, pieces):
        queries = inbox[p].reshape(half, -1)
        scores, onehots = [], []
        for _, xx, col, quarter in pieces:
            at = pl.ds(pl.multiple_of(quarter * qrows, qrows), qrows)
            keys = kbuf[p, xx * 2 + col, at, :]
            named = lab[xx * 2 + col, pl.ds(p, 1), at]
            classes = lax.broadcasted_iota(jnp.int32, (NCLASS, qrows), 0)
            onehots.append(jnp.where(classes == named, 1.0, 0.0).astype(jnp.bfloat16))
            scores.append(lax.dot_general(queries, keys, NT, preferred_element_type=jnp.float32))
        scores = jnp.concatenate(scores, axis=1)
        m_old = m_s[p]
        m_new = jnp.maximum(m_old, jnp.max(scores, axis=1, keepdims=True))
        m_s[p] = m_new
        fade = jnp.exp2((m_old - m_new) * log2e)
        wide = jnp.concatenate([m_new] * (scores.shape[1] // 128), axis=1)
        weights = jnp.exp2((scores - wide) * log2e)
        high = weights.astype(jnp.bfloat16)
        low = (weights - high.astype(jnp.float32)).astype(jnp.bfloat16)
        sums = lax.dot_general(
            jnp.concatenate([high, low], axis=1), jnp.concatenate(onehots * 2, axis=1), NT,
            preferred_element_type=jnp.float32,
        )
        acc[p] = acc[p] * fade + sums

    def own_unit(t, carry):
        p, i = lax.div(t, 2), lax.rem(t, 2)
        col = lax.rem(c + i, 2)
        pl.when(t >= 2)(lambda: event(t + 1))

        @pl.when(i == 1)
        def _():
            ref = kbuf.at[p, x * 2 + col]
            pltpu.make_async_copy(ref, ref, so_r.at[p]).wait()

        unit(p, [(p, x, col, quarter) for quarter in range(4)])
        return carry

    def passed(g):
        for way in range(2):
            ref = piece(*landed(way, g, 1 - c))
            pltpu.make_async_copy(ref, ref, bs_r.at[way, g]).wait()

    def ring_unit(g, carry):
        pl.when(g == 1)(lambda: event(5))
        pl.when(g == 4)(lambda: event(6))
        pl.when(g >= 6)(lambda: event(g + 1))

        @pl.when(g == 6)
        def _():
            finish(0)
            send_back(0)

        passed(g)
        unit(lax.div(g, 6), [landed(way, g, col) for col in (c, 1 - c) for way in range(2)])
        return carry

    def last_unit(t, carry):
        g, i = 10 + lax.div(t, 2), lax.rem(t, 2)
        pl.when(t == 1)(lambda: event(11))
        pl.when(i == 1)(lambda: passed(g))
        unit(PARTS - 1, [landed(way, g, lax.rem(c + i, 2)) for way in range(2)])
        return carry

    def finish(p):
        lane = lax.broadcasted_iota(jnp.int32, (half, 128), 1) % CAP
        slot = lax.broadcasted_iota(jnp.int32, (half, 128), 0) % CAP
        diag = jnp.where(lane == slot, m_s[p], 0.0).reshape(nd, CAP, 128)
        mout[p, :, 0] = jnp.sum(diag, axis=1, keepdims=True)
        sums = acc[p]
        most = jnp.max(sums, axis=1, keepdims=True)
        diag = jnp.where(lane == slot, most, 0.0).reshape(nd, CAP, 128)
        mout[p, :, 1] = jnp.sum(diag, axis=1, keepdims=True)
        codes = jnp.round(sums * (STEPS / most)).astype(jnp.int32).astype(jnp.int16)
        wire[p] = codes.reshape(nd, CAP, NCLASS)

    def send_back(p):
        to_all(lambda d: wire.at[p, d], lambda d: ret.at[p, d], rs.at[p], rr.at[p])
        to_all(lambda d: mout.at[p, d], lambda d: pin.at[p, d], ps.at[p], pr.at[p])

    event(0)
    event(1)
    share_own(1).start()
    m_s[...] = jnp.full(m_s.shape, -3.0e38, jnp.float32)
    acc[...] = jnp.zeros(acc.shape, jnp.float32)
    mask[...] = sel.T
    pltpu.make_async_copy(lab.at[pl.ds(0, nrep - 1)], lab.at[pl.ds(0, nrep - 1)], lr).wait()
    event(2)
    pltpu.make_async_copy(inbox, inbox, qr).wait()
    lax.fori_loop(0, 4, own_unit, 0)
    lax.fori_loop(0, 10, ring_unit, 0)
    lax.fori_loop(0, 4, last_unit, 0)
    finish(1)
    send_back(1)

    def gone(g, carry):
        for way in range(2):
            ring(way, g).wait_send()
            share(way, g).wait_send()
        return carry

    lax.fori_loop(0, 12, gone, 0)
    for p in range(PARTS):
        share_own(p).wait_send()
    others = pl.ds(0, nd - 1)
    few = pl.ds(0, nrep - 1)
    pltpu.make_async_copy(outbox.at[:, others], outbox.at[:, others], qs).wait()
    pltpu.make_async_copy(lab.at[few], lab.at[few], ls).wait()

    def left_home(p):
        pltpu.make_async_copy(wire.at[p, others], wire.at[p, others], rs.at[p]).wait()
        pltpu.make_async_copy(mout.at[p, others], mout.at[p, others], ps.at[p]).wait()

    left_home(0)

    nq = q_ref.shape[0]
    per = 128 // CAP
    lane = lax.broadcasted_iota(jnp.int32, (1, 128), 1) // CAP
    top = jnp.full((nq, 1), -3.0e38, jnp.float32)
    total = jnp.zeros((nq, NCLASS), jnp.float32)
    for p in range(PARTS):
        pltpu.make_async_copy(pin.at[p], pin.at[p], pr.at[p]).wait()
        found = []
        new_top = top
        for g in range(half // 128):
            line = jnp.zeros((1, 128), jnp.float32)
            most = jnp.zeros((1, 128), jnp.float32)
            for i in range(per):
                line = jnp.where(lane == i, pin[p, g * per + i, 0], line)
                most = jnp.where(lane == i, pin[p, g * per + i, 1], most)
            chosen = mask[:, p * half + g * 128 : p * half + (g + 1) * 128] > 0.0
            found.append((chosen, line, most))
            best = jnp.max(jnp.where(chosen, line, -3.0e38), axis=1, keepdims=True)
            new_top = jnp.maximum(new_top, best)
        total = total * jnp.exp2((top - new_top) * log2e)
        top = new_top
        factors = [
            jnp.where(chosen, jnp.exp2(jnp.where(chosen, line - top, 0.0) * log2e) * (most / STEPS), 0.0)
            for chosen, line, most in found
        ]
        pltpu.make_async_copy(ret.at[p], ret.at[p], rr.at[p]).wait()
        codes = ret[p].astype(jnp.int32).astype(jnp.float32).reshape(half, NCLASS)
        total += jnp.dot(
            jnp.concatenate(factors, axis=1), codes,
            precision=lax.Precision.HIGHEST, preferred_element_type=jnp.float32,
        )
    out_ref[...] = NCLASS * total / jnp.sum(total, axis=1, keepdims=True)
    left_home(1)


def local(queries, probes, corpus, labels):
    nd = lax.axis_size("dom")
    nrep = lax.axis_size("rep")
    nq, depth = queries.shape
    rows = corpus.shape[1]
    half = nd * CAP
    dma = pltpu.SemaphoreType.DMA
    return pl.pallas_call(
        functools.partial(kernel, nd, nrep // 2),
        out_shape=jax.ShapeDtypeStruct((nq, NCLASS), jnp.float32),
        in_specs=[pl.BlockSpec(memory_space=pl.ANY)] * 4,
        out_specs=pl.BlockSpec(memory_space=pltpu.VMEM),
        scratch_shapes=[
            pltpu.VMEM((nq, depth), jnp.bfloat16),
            pltpu.VMEM((probes.shape[1], nq), jnp.int32),
            pltpu.VMEM((nq, PARTS * half), jnp.float32),
            pltpu.VMEM((PARTS, nd, CAP, depth), jnp.bfloat16),
            pltpu.VMEM((PARTS, nd, CAP, depth), jnp.bfloat16),
            pltpu.VMEM((PARTS, nrep, rows, depth), jnp.bfloat16),
            pltpu.VMEM((nrep, PARTS, rows), jnp.int32),
            pltpu.VMEM((PARTS, half, NCLASS), jnp.float32),
            pltpu.VMEM((PARTS, half, 128), jnp.float32),
            pltpu.VMEM((PARTS, nd, CAP, NCLASS), jnp.int16),
            pltpu.VMEM((PARTS, nd, 2, 1, 128), jnp.float32),
            pltpu.VMEM((PARTS, nd, 2, 1, 128), jnp.float32),
            pltpu.VMEM((PARTS, nd, CAP, NCLASS), jnp.int16),
            dma((3,)),
            dma((PARTS,)),
            dma((PARTS,)),
            dma((PARTS,)),
            dma((2, 12)),
            dma((2, 12)),
            dma((2, 12)),
            dma((2, 12)),
            dma, dma, dma, dma,
            dma((PARTS,)),
            dma((PARTS,)),
            dma((PARTS,)),
            dma((PARTS,)),
        ],
        compiler_params=pltpu.CompilerParams(
            collective_id=0, has_side_effects=True, vmem_limit_bytes=62 * 1024 * 1024
        ),
    )(queries, probes.T, corpus, labels)


def solution(mesh):
    in_specs = (
        P(("dom", "rep"), None),
        P(("dom", "rep"), None),
        P("dom", "rep", None),
        P("dom", "rep"),
    )
    out_specs = P(("dom", "rep"), None)
    return jax.shard_map(local, mesh=mesh, in_specs=in_specs, out_specs=out_specs, check_vma=False)
```

```python
import functools
import math

import jax
import jax.numpy as jnp
from jax import lax
from jax.experimental import pallas as pl
from jax.experimental.pallas import tpu as pltpu
from jax.sharding import PartitionSpec as P

NCLASS = 128
CAP = 16
PARTS = 2
WINDOW = 4
STEPS = 32767.0
MESH = pl.DeviceIdType.MESH
NT = (((1,), (1,)), ((), ()))


def select_slots(named, nd):
    npr, nq = named.shape
    nparts = PARTS * nd
    width = max(128, nparts)
    part_ids = lax.broadcasted_iota(jnp.int32, (width, nq), 0)
    match = jnp.zeros((width, nq), jnp.float32)
    for j in range(npr):
        match = jnp.where(named[j : j + 1, :] == part_ids, 1.0, match)
    row = lax.broadcasted_iota(jnp.int32, (nq, nq), 0)
    col = lax.broadcasted_iota(jnp.int32, (nq, nq), 1)
    earlier = jnp.where(row < col, 1.0, 0.0).astype(jnp.bfloat16)
    rank = jnp.dot(match.astype(jnp.bfloat16), earlier, preferred_element_type=jnp.float32)
    code = jnp.where(match > 0.0, rank, -1.0)
    slots = nparts * CAP
    half = nd * CAP
    slot_row = lax.broadcasted_iota(jnp.int32, (slots, width), 0)
    slot_part = PARTS * ((slot_row % half) // CAP) + slot_row // half
    spread = jnp.where(lax.broadcasted_iota(jnp.int32, (slots, width), 1) == slot_part, 1.0, 0.0)
    wide = jnp.dot(
        spread.astype(jnp.bfloat16), code.astype(jnp.bfloat16), preferred_element_type=jnp.float32
    )
    slot = (lax.broadcasted_iota(jnp.int32, (slots, nq), 0) % CAP).astype(jnp.float32)
    return jnp.where(wide == slot, 1.0, 0.0)


def kernel(
    nd, nx,
    q_hbm, probes_hbm, corpus_hbm, labels_hbm, out_ref,
    q_ref, probes_ref, mask, outbox, inbox, kbuf, lab, acc, m_s, wire, mout, pin, ret,
    fs, ko, so_s, so_r, ks, kr, bs_s, bs_r, ls_s, ls_r, lb_s, lb_r, qs, qr, ls, lr, ms, mr, rs, rr, ps, pr,
):
    dom = lax.axis_index("dom")
    rep = lax.axis_index("rep")
    x, c = lax.div(rep, 2), lax.rem(rep, 2)
    rows = kbuf.shape[2]
    qrows = rows // 4
    hrows = rows // 8
    half = nd * CAP
    nz = min(nd, 8)
    ny = nd // nz
    y, z = lax.div(dom, nz), lax.rem(dom, nz)
    right = (dom, lax.rem(x + 1, nx) * 2 + c)
    left = (dom, lax.rem(x + nx - 1, nx) * 2 + c)
    across = (dom, lax.rem(x + 2, nx) * 2 + c)
    sibling = (dom, x * 2 + (1 - c))

    lines = [
        lax.rem(y + (ny // 2 + (1 - 2 * (j % 2)) * ((j + 1) // 2)), ny) * nz for j in range(ny)
    ]

    def each_peer(act):
        def one(i, carry):
            dz = nz // 2 + (1 - 2 * lax.rem(i, 2)) * lax.div(i + 1, 2)
            there = lax.rem(z + dz, nz)
            for line in lines:
                act(line + there)
            return carry

        lax.fori_loop(0, nz - 1, one, 0)
        for line in lines[:-1]:
            act(line + z)

    barrier = pltpu.get_barrier_semaphore()

    def greet(device):
        pl.semaphore_signal(barrier, inc=1, device_id=device, device_id_type=MESH)

    for device in (sibling, right, left, across):
        greet(device)
    each_peer(lambda peer: greet((peer, rep)))

    get_probes = pltpu.make_async_copy(probes_hbm, probes_ref, fs.at[0])
    get_queries = pltpu.make_async_copy(q_hbm, q_ref, fs.at[1])
    get_labels = pltpu.make_async_copy(labels_hbm, lab.at[rep], fs.at[2])
    get_rows = [
        pltpu.make_async_copy(corpus_hbm.at[p], kbuf.at[p, rep], ko.at[p]) for p in range(PARTS)
    ]
    for copy in (get_probes, get_queries, get_rows[0], get_labels, get_rows[1]):
        copy.start()
    get_rows[0].wait()

    pl.semaphore_wait(barrier, nd + 3)

    def piece(p, xx, col, quarter):
        return kbuf.at[p, xx * 2 + col, pl.ds(pl.multiple_of(quarter * qrows, qrows), qrows)]

    def ring(way, g):
        p, k = lax.div(g, 6), lax.rem(g, 6)
        if way == 0:
            ref = piece(p, lax.rem(x + nx - lax.div(k, 4), nx), c, lax.rem(k, 4))
        else:
            ref = piece(p, lax.rem(x + lax.div(k, 4), nx), c, 3 - lax.rem(k, 4))
        return pltpu.make_async_remote_copy(
            src_ref=ref, dst_ref=ref, send_sem=ks.at[way, g], recv_sem=kr.at[way, g],
            device_id=right if way == 0 else left, device_id_type=MESH,
        )

    def landed(way, g, col):
        p, k = lax.div(g, 6), lax.rem(g, 6)
        if way == 0:
            return p, lax.rem(x + 2 * nx - 1 - lax.div(k, 4), nx), col, lax.rem(k, 4)
        return p, lax.rem(x + 1 + lax.div(k, 4), nx), col, 3 - lax.rem(k, 4)

    def share(way, g):
        ref = piece(*landed(way, g, c))
        return pltpu.make_async_remote_copy(
            src_ref=ref, dst_ref=ref, send_sem=bs_s.at[way, g], recv_sem=bs_r.at[way, g],
            device_id=sibling, device_id_type=MESH,
        )

    def halves(way, col):
        p, xx, col, quarter = landed(way, 11, col)
        return [
            kbuf.at[p, xx * 2 + col, pl.ds(pl.multiple_of(quarter * qrows + j * hrows, hrows), hrows)]
            for j in range(2)
        ]

    def last_ring(way, j):
        p, xx, quarter = PARTS - 1, lax.rem(x + (nx - 1 if way == 0 else 1), nx), 1 if way == 0 else 2
        ref = kbuf.at[p, xx * 2 + c, pl.ds(quarter * qrows + j * hrows, hrows)]
        return pltpu.make_async_remote_copy(
            src_ref=ref, dst_ref=ref, send_sem=ls_s.at[way, j], recv_sem=ls_r.at[way, j],
            device_id=right if way == 0 else left, device_id_type=MESH,
        )

    def last_share(way, j):
        ref = halves(way, c)[j]
        return pltpu.make_async_remote_copy(
            src_ref=ref, dst_ref=ref, send_sem=lb_s.at[way, j], recv_sem=lb_r.at[way, j],
            device_id=sibling, device_id_type=MESH,
        )

    def share_own(p):
        ref = kbuf.at[p, rep]
        return pltpu.make_async_remote_copy(
            src_ref=ref, dst_ref=ref, send_sem=so_s.at[p], recv_sem=so_r.at[p],
            device_id=sibling, device_id_type=MESH,
        )

    for g in range(WINDOW):
        ring(0, g).start()
        ring(1, g).start()

    get_probes.wait()
    get_queries.wait()
    sel = select_slots(probes_ref[...], nd)
    picked = jnp.dot(sel.astype(jnp.bfloat16), q_ref[...], preferred_element_type=jnp.float32)
    outbox[...] = picked.astype(jnp.bfloat16).reshape(outbox.shape)
    get_labels.wait()
    get_rows[1].wait()


    def to_all(*blocks):
        def send(peer):
            for src, dst, send_sem, recv_sem in blocks:
                pltpu.make_async_remote_copy(
                    src_ref=src(peer), dst_ref=dst(dom), send_sem=send_sem, recv_sem=recv_sem,
                    device_id=(peer, rep), device_id_type=MESH,
                ).start()

        each_peer(send)
        for src, dst, _, recv_sem in blocks:
            pltpu.make_async_copy(src(dom), dst(dom), recv_sem).start()

    to_all((lambda d: outbox.at[:, d], lambda d: inbox.at[:, d], qs, qr))

    def send_label(xx, device, send_sem, recv_sem):
        ref = lab.at[xx * 2 + c]
        pltpu.make_async_remote_copy(
            src_ref=ref, dst_ref=ref, send_sem=send_sem, recv_sem=recv_sem,
            device_id=device, device_id_type=MESH,
        ).start()

    for device in (right, left, across):
        send_label(x, device, ls, lr)
    send_label(x, sibling, ms, mr)
    share_own(0).start()

    def event(g):
        for way in range(2):
            ref = piece(*landed(way, g, c))
            pltpu.make_async_copy(ref, ref, kr.at[way, g]).wait()
            share(way, g).start()

        for way in range(2):
            if g + WINDOW < 11:
                ring(way, g + WINDOW).start()
            elif g + WINDOW == 11:
                last_ring(way, 0).start()
                last_ring(way, 1).start()

    def last_event(j):
        for way in range(2):
            ref = halves(way, c)[j]
            pltpu.make_async_copy(ref, ref, ls_r.at[way, j]).wait()
            last_share(way, j).start()

    log2e = math.log2(math.e) * (q_ref.shape[1] ** -0.5)

    def unit(p, pieces, cut=None):
        queries = inbox[p].reshape(half, -1)
        scores, onehots = [], []
        for _, xx, col, quarter in pieces:
            size, start = qrows, quarter * qrows
            if cut is not None:
                size, start = hrows, start + cut * hrows
            at = pl.ds(pl.multiple_of(start, size), size)
            keys = kbuf[p, xx * 2 + col, at, :]
            named = lab[xx * 2 + col, pl.ds(p, 1), at]
            classes = lax.broadcasted_iota(jnp.int32, (NCLASS, size), 0)
            onehots.append(jnp.where(classes == named, 1.0, 0.0).astype(jnp.bfloat16))
            scores.append(lax.dot_general(queries, keys, NT, preferred_element_type=jnp.float32))
        scores = jnp.concatenate(scores, axis=1)
        m_old = m_s[p]
        m_new = jnp.maximum(m_old, jnp.max(scores, axis=1, keepdims=True))
        m_s[p] = m_new
        fade = jnp.exp2((m_old - m_new) * log2e)
        wide = jnp.concatenate([m_new] * (scores.shape[1] // 128), axis=1)
        weights = jnp.exp2((scores - wide) * log2e)
        high = weights.astype(jnp.bfloat16)
        low = (weights - high.astype(jnp.float32)).astype(jnp.bfloat16)
        sums = lax.dot_general(
            jnp.concatenate([high, low], axis=1), jnp.concatenate(onehots * 2, axis=1), NT,
            preferred_element_type=jnp.float32,
        )
        acc[p] = acc[p] * fade + sums

    def own_unit(t, carry):
        p, i = lax.div(t, 2), lax.rem(t, 2)
        col = lax.rem(c + i, 2)
        pl.when(t == 2)(lambda: event(3))
        pl.when(t == 3)(lambda: event(4))

        @pl.when(i == 1)
        def _():
            ref = kbuf.at[p, x * 2 + col]
            pltpu.make_async_copy(ref, ref, so_r.at[p]).wait()

        unit(p, [(p, x, col, quarter) for quarter in range(4)])
        return carry

    def passed(g):
        for way in range(2):
            ref = piece(*landed(way, g, 1 - c))
            pltpu.make_async_copy(ref, ref, bs_r.at[way, g]).wait()

    def ring_unit(g, carry):
        for at, turn in ((1, 5), (4, 6), (6, 7), (7, 8), (8, 9), (9, 10)):
            pl.when(g == at)(functools.partial(event, turn))

        @pl.when(g == 6)
        def _():
            finish(0)
            send_back(0)

        passed(g)
        unit(lax.div(g, 6), [landed(way, g, col) for col in (c, 1 - c) for way in range(2)])
        return carry

    def late_unit(t, carry):
        g, i = 10 + lax.div(t, 2), lax.rem(t, 2)

        @pl.when(t == 1)
        def _():
            last_event(0)
            passed(g)

        pl.when(t == 2)(lambda: last_event(1))
        unit(PARTS - 1, [landed(way, g, lax.rem(c + i, 2)) for way in range(2)])
        return carry

    def last_unit(j, carry):
        for way in range(2):
            p, xx, col, quarter = landed(way, 11, 1 - c)
            start = pl.multiple_of(quarter * qrows + j * hrows, hrows)
            ref = kbuf.at[p, xx * 2 + col, pl.ds(start, hrows)]
            pltpu.make_async_copy(ref, ref, lb_r.at[way, j]).wait()
        unit(PARTS - 1, [landed(way, 11, 1 - c) for way in range(2)], j)
        return carry

    def finish(p):
        lane = lax.broadcasted_iota(jnp.int32, (half, 128), 1) % CAP
        slot = lax.broadcasted_iota(jnp.int32, (half, 128), 0) % CAP
        diag = jnp.where(lane == slot, m_s[p], 0.0).reshape(nd, CAP, 128)
        mout[p, :, 0] = jnp.sum(diag, axis=1, keepdims=True)
        sums = acc[p]
        most = jnp.max(sums, axis=1, keepdims=True)
        diag = jnp.where(lane == slot, most, 0.0).reshape(nd, CAP, 128)
        mout[p, :, 1] = jnp.sum(diag, axis=1, keepdims=True)
        codes = jnp.round(sums * (STEPS / most)).astype(jnp.int32).astype(jnp.int16)
        wire[p] = codes.reshape(nd, CAP, NCLASS)

    def send_back(p):
        to_all(
            (lambda d: mout.at[p, d], lambda d: pin.at[p, d], ps.at[p], pr.at[p]),
            (lambda d: wire.at[p, d], lambda d: ret.at[p, d], rs.at[p], rr.at[p]),
        )

    event(0)
    far = pl.ds(0, nx - 1)
    pltpu.make_async_copy(lab.at[far], lab.at[far], lr).wait()
    for k in range(1, nx):
        send_label(lax.rem(x + k, nx), sibling, ms, mr)
    event(1)
    share_own(1).start()
    m_s[...] = jnp.full(m_s.shape, -3.0e38, jnp.float32)
    acc[...] = jnp.zeros(acc.shape, jnp.float32)
    mask[...] = sel.T
    few = pl.ds(0, nx)
    pltpu.make_async_copy(lab.at[few], lab.at[few], mr).wait()
    event(2)
    pltpu.make_async_copy(inbox, inbox, qr).wait()
    lax.fori_loop(0, 4, own_unit, 0)
    lax.fori_loop(0, 10, ring_unit, 0)
    lax.fori_loop(0, 3, late_unit, 0)
    lax.fori_loop(0, 2, last_unit, 0)
    finish(1)
    send_back(1)

    def gone(g, carry):
        for way in range(2):
            ring(way, g).wait_send()
            share(way, g).wait_send()
        return carry

    lax.fori_loop(0, 11, gone, 0)
    for way in range(2):
        for j in range(2):
            last_ring(way, j).wait_send()
            last_share(way, j).wait_send()
    for p in range(PARTS):
        share_own(p).wait_send()
    others = pl.ds(0, nd - 1)
    pltpu.make_async_copy(outbox.at[:, others], outbox.at[:, others], qs).wait()
    pltpu.make_async_copy(lab.at[far], lab.at[far], ls).wait()
    pltpu.make_async_copy(lab.at[few], lab.at[few], ms).wait()

    def left_home(p):
        pltpu.make_async_copy(wire.at[p, others], wire.at[p, others], rs.at[p]).wait()
        pltpu.make_async_copy(mout.at[p, others], mout.at[p, others], ps.at[p]).wait()

    left_home(0)

    nq = q_ref.shape[0]
    per = 128 // CAP
    lane = lax.broadcasted_iota(jnp.int32, (1, 128), 1) // CAP
    top = jnp.full((nq, 1), -3.0e38, jnp.float32)
    total = jnp.zeros((nq, NCLASS), jnp.float32)
    for p in range(PARTS):
        pltpu.make_async_copy(pin.at[p], pin.at[p], pr.at[p]).wait()
        found = []
        new_top = top
        for g in range(half // 128):
            line = jnp.zeros((1, 128), jnp.float32)
            most = jnp.zeros((1, 128), jnp.float32)
            for i in range(per):
                line = jnp.where(lane == i, pin[p, g * per + i, 0], line)
                most = jnp.where(lane == i, pin[p, g * per + i, 1], most)
            chosen = mask[:, p * half + g * 128 : p * half + (g + 1) * 128] > 0.0
            found.append((chosen, line, most))
            best = jnp.max(jnp.where(chosen, line, -3.0e38), axis=1, keepdims=True)
            new_top = jnp.maximum(new_top, best)
        total = total * jnp.exp2((top - new_top) * log2e)
        top = new_top
        factors = [
            jnp.where(chosen, jnp.exp2(jnp.where(chosen, line - top, 0.0) * log2e) * (most / STEPS), 0.0)
            for chosen, line, most in found
        ]
        pltpu.make_async_copy(ret.at[p], ret.at[p], rr.at[p]).wait()
        codes = ret[p].astype(jnp.int32).astype(jnp.float32).reshape(half, NCLASS)
        total += jnp.dot(
            jnp.concatenate(factors, axis=1), codes,
            precision=lax.Precision.HIGHEST, preferred_element_type=jnp.float32,
        )
    out_ref[...] = NCLASS * total / jnp.sum(total, axis=1, keepdims=True)
    left_home(1)


def local(queries, probes, corpus, labels):
    nd = lax.axis_size("dom")
    nrep = lax.axis_size("rep")
    nq, depth = queries.shape
    rows = corpus.shape[1]
    half = nd * CAP
    dma = pltpu.SemaphoreType.DMA
    return pl.pallas_call(
        functools.partial(kernel, nd, nrep // 2),
        out_shape=jax.ShapeDtypeStruct((nq, NCLASS), jnp.float32),
        in_specs=[pl.BlockSpec(memory_space=pl.ANY)] * 4,
        out_specs=pl.BlockSpec(memory_space=pltpu.VMEM),
        scratch_shapes=[
            pltpu.VMEM((nq, depth), jnp.bfloat16),
            pltpu.VMEM((probes.shape[1], nq), jnp.int32),
            pltpu.VMEM((nq, PARTS * half), jnp.float32),
            pltpu.VMEM((PARTS, nd, CAP, depth), jnp.bfloat16),
            pltpu.VMEM((PARTS, nd, CAP, depth), jnp.bfloat16),
            pltpu.VMEM((PARTS, nrep, rows, depth), jnp.bfloat16),
            pltpu.VMEM((nrep, PARTS, rows), jnp.int32),
            pltpu.VMEM((PARTS, half, NCLASS), jnp.float32),
            pltpu.VMEM((PARTS, half, 128), jnp.float32),
            pltpu.VMEM((PARTS, nd, CAP, NCLASS), jnp.int16),
            pltpu.VMEM((PARTS, nd, 2, 1, 128), jnp.float32),
            pltpu.VMEM((PARTS, nd, 2, 1, 128), jnp.float32),
            pltpu.VMEM((PARTS, nd, CAP, NCLASS), jnp.int16),
            dma((3,)),
            dma((PARTS,)),
            dma((PARTS,)),
            dma((PARTS,)),
            dma((2, 11)),
            dma((2, 11)),
            dma((2, 11)),
            dma((2, 11)),
            dma((2, 2)),
            dma((2, 2)),
            dma((2, 2)),
            dma((2, 2)),
            dma, dma, dma, dma, dma, dma,
            dma((PARTS,)),
            dma((PARTS,)),
            dma((PARTS,)),
            dma((PARTS,)),
        ],
        compiler_params=pltpu.CompilerParams(
            collective_id=0, has_side_effects=True, vmem_limit_bytes=62 * 1024 * 1024
        ),
    )(queries, probes.T, corpus, labels)


def solution(mesh):
    in_specs = (
        P(("dom", "rep"), None),
        P(("dom", "rep"), None),
        P("dom", "rep", None),
        P("dom", "rep"),
    )
    out_specs = P(("dom", "rep"), None)
    return jax.shard_map(local, mesh=mesh, in_specs=in_specs, out_specs=out_specs, check_vma=False)
```

```python
import functools
import math

import jax
import jax.numpy as jnp
from jax import lax
from jax.experimental import pallas as pl
from jax.experimental.pallas import tpu as pltpu
from jax.sharding import PartitionSpec as P

NCLASS = 128
CAP = 16
PARTS = 2
WINDOW = 4
STEPS = 32767.0
MESH = pl.DeviceIdType.MESH
NT = (((1,), (1,)), ((), ()))


def select_slots(named, nd):
    npr, nq = named.shape
    nparts = PARTS * nd
    width = max(128, nparts)
    part_ids = lax.broadcasted_iota(jnp.int32, (width, nq), 0)
    match = jnp.zeros((width, nq), jnp.float32)
    for j in range(npr):
        match = jnp.where(named[j : j + 1, :] == part_ids, 1.0, match)
    row = lax.broadcasted_iota(jnp.int32, (nq, nq), 0)
    col = lax.broadcasted_iota(jnp.int32, (nq, nq), 1)
    earlier = jnp.where(row < col, 1.0, 0.0).astype(jnp.bfloat16)
    rank = jnp.dot(match.astype(jnp.bfloat16), earlier, preferred_element_type=jnp.float32)
    code = jnp.where(match > 0.0, rank, -1.0)
    slots = nparts * CAP
    half = nd * CAP
    slot_row = lax.broadcasted_iota(jnp.int32, (slots, width), 0)
    slot_part = PARTS * ((slot_row % half) // CAP) + slot_row // half
    spread = jnp.where(lax.broadcasted_iota(jnp.int32, (slots, width), 1) == slot_part, 1.0, 0.0)
    wide = jnp.dot(
        spread.astype(jnp.bfloat16), code.astype(jnp.bfloat16), preferred_element_type=jnp.float32
    )
    slot = (lax.broadcasted_iota(jnp.int32, (slots, nq), 0) % CAP).astype(jnp.float32)
    return jnp.where(wide == slot, 1.0, 0.0)


def kernel(
    nd, nx,
    q_hbm, probes_hbm, corpus_hbm, labels_hbm, out_ref,
    q_ref, probes_ref, mask, outbox, inbox, kbuf, lab, acc, m_s, wire, mout, pin, ret,
    fs, ko, so_s, so_r, ks, kr, bs_s, bs_r, ls_s, ls_r, lb_s, lb_r, qs, qr, ls, lr, ms, mr, rs, rr, ps, pr,
):
    dom = lax.axis_index("dom")
    rep = lax.axis_index("rep")
    x, c = lax.div(rep, 2), lax.rem(rep, 2)
    rows = kbuf.shape[2]
    qrows = rows // 4
    hrows = rows // 8
    half = nd * CAP
    nz = min(nd, 8)
    ny = nd // nz
    y, z = lax.div(dom, nz), lax.rem(dom, nz)
    right = (dom, lax.rem(x + 1, nx) * 2 + c)
    left = (dom, lax.rem(x + nx - 1, nx) * 2 + c)
    across = (dom, lax.rem(x + 2, nx) * 2 + c)
    sibling = (dom, x * 2 + (1 - c))

    lines = [
        lax.rem(y + (ny // 2 + (1 - 2 * (j % 2)) * ((j + 1) // 2)), ny) * nz for j in range(ny)
    ]

    def each_peer(act):
        def one(i, carry):
            dz = nz // 2 + (1 - 2 * lax.rem(i, 2)) * lax.div(i + 1, 2)
            there = lax.rem(z + dz, nz)
            for line in lines:
                act(line + there)
            return carry

        lax.fori_loop(0, nz - 1, one, 0)
        for line in lines[:-1]:
            act(line + z)

    barrier = pltpu.get_barrier_semaphore()

    def greet(device):
        pl.semaphore_signal(barrier, inc=1, device_id=device, device_id_type=MESH)

    for device in (sibling, right, left, across):
        greet(device)
    each_peer(lambda peer: greet((peer, rep)))

    get_probes = pltpu.make_async_copy(probes_hbm, probes_ref, fs.at[0])
    get_queries = pltpu.make_async_copy(q_hbm, q_ref, fs.at[1])
    get_labels = pltpu.make_async_copy(labels_hbm, lab.at[rep], fs.at[2])
    get_rows = [
        pltpu.make_async_copy(corpus_hbm.at[p], kbuf.at[p, rep], ko.at[p]) for p in range(PARTS)
    ]
    for copy in (get_probes, get_queries, get_rows[0], get_labels, get_rows[1]):
        copy.start()
    get_rows[0].wait()

    pl.semaphore_wait(barrier, nd + 3)

    def piece(p, xx, col, quarter):
        return kbuf.at[p, xx * 2 + col, pl.ds(pl.multiple_of(quarter * qrows, qrows), qrows)]

    def ring(way, g):
        p, k = lax.div(g, 6), lax.rem(g, 6)
        if way == 0:
            ref = piece(p, lax.rem(x + nx - lax.div(k, 4), nx), c, lax.rem(k, 4))
        else:
            ref = piece(p, lax.rem(x + lax.div(k, 4), nx), c, 3 - lax.rem(k, 4))
        return pltpu.make_async_remote_copy(
            src_ref=ref, dst_ref=ref, send_sem=ks.at[way, g], recv_sem=kr.at[way, g],
            device_id=right if way == 0 else left, device_id_type=MESH,
        )

    def landed(way, g, col):
        p, k = lax.div(g, 6), lax.rem(g, 6)
        if way == 0:
            return p, lax.rem(x + 2 * nx - 1 - lax.div(k, 4), nx), col, lax.rem(k, 4)
        return p, lax.rem(x + 1 + lax.div(k, 4), nx), col, 3 - lax.rem(k, 4)

    def share(way, g):
        ref = piece(*landed(way, g, c))
        return pltpu.make_async_remote_copy(
            src_ref=ref, dst_ref=ref, send_sem=bs_s.at[way, g], recv_sem=bs_r.at[way, g],
            device_id=sibling, device_id_type=MESH,
        )

    def halves(way, col):
        p, xx, col, quarter = landed(way, 11, col)
        return [
            kbuf.at[p, xx * 2 + col, pl.ds(pl.multiple_of(quarter * qrows + j * hrows, hrows), hrows)]
            for j in range(2)
        ]

    def last_ring(way, j):
        p, xx, quarter = PARTS - 1, lax.rem(x + (nx - 1 if way == 0 else 1), nx), 1 if way == 0 else 2
        ref = kbuf.at[p, xx * 2 + c, pl.ds(quarter * qrows + j * hrows, hrows)]
        return pltpu.make_async_remote_copy(
            src_ref=ref, dst_ref=ref, send_sem=ls_s.at[way, j], recv_sem=ls_r.at[way, j],
            device_id=right if way == 0 else left, device_id_type=MESH,
        )

    def last_share(way, j):
        ref = halves(way, c)[j]
        return pltpu.make_async_remote_copy(
            src_ref=ref, dst_ref=ref, send_sem=lb_s.at[way, j], recv_sem=lb_r.at[way, j],
            device_id=sibling, device_id_type=MESH,
        )

    def share_own(p):
        ref = kbuf.at[p, rep]
        return pltpu.make_async_remote_copy(
            src_ref=ref, dst_ref=ref, send_sem=so_s.at[p], recv_sem=so_r.at[p],
            device_id=sibling, device_id_type=MESH,
        )

    for g in range(WINDOW):
        ring(0, g).start()
        ring(1, g).start()

    get_probes.wait()
    get_queries.wait()
    sel = select_slots(probes_ref[...], nd)
    picked = jnp.dot(sel.astype(jnp.bfloat16), q_ref[...], preferred_element_type=jnp.float32)
    outbox[...] = picked.astype(jnp.bfloat16).reshape(outbox.shape)
    get_labels.wait()
    get_rows[1].wait()


    def to_all(*blocks):
        def send(peer):
            for src, dst, send_sem, recv_sem in blocks:
                pltpu.make_async_remote_copy(
                    src_ref=src(peer), dst_ref=dst(dom), send_sem=send_sem, recv_sem=recv_sem,
                    device_id=(peer, rep), device_id_type=MESH,
                ).start()

        each_peer(send)
        for src, dst, _, recv_sem in blocks:
            pltpu.make_async_copy(src(dom), dst(dom), recv_sem).start()

    to_all((lambda d: outbox.at[:, d], lambda d: inbox.at[:, d], qs, qr))

    def send_label(xx, device, send_sem, recv_sem):
        ref = lab.at[xx * 2 + c]
        pltpu.make_async_remote_copy(
            src_ref=ref, dst_ref=ref, send_sem=send_sem, recv_sem=recv_sem,
            device_id=device, device_id_type=MESH,
        ).start()

    for device in (right, left, across):
        send_label(x, device, ls, lr)
    send_label(x, sibling, ms, mr)
    share_own(0).start()

    def event(g):
        for way in range(2):
            ref = piece(*landed(way, g, c))
            pltpu.make_async_copy(ref, ref, kr.at[way, g]).wait()
            share(way, g).start()

        for way in range(2):
            if g + WINDOW < 11:
                ring(way, g + WINDOW).start()
            elif g + WINDOW == 11:
                last_ring(way, 0).start()
                last_ring(way, 1).start()

    def last_event(j):
        for way in range(2):
            ref = halves(way, c)[j]
            pltpu.make_async_copy(ref, ref, ls_r.at[way, j]).wait()
            last_share(way, j).start()

    log2e = math.log2(math.e) * (q_ref.shape[1] ** -0.5)

    def unit(p, pieces, cut=None):
        queries = inbox[p].reshape(half, -1)
        scores, onehots = [], []
        for _, xx, col, quarter in pieces:
            size, start = qrows, quarter * qrows
            if cut is not None:
                size, start = hrows, start + cut * hrows
            at = pl.ds(pl.multiple_of(start, size), size)
            keys = kbuf[p, xx * 2 + col, at, :]
            named = lab[xx * 2 + col, pl.ds(p, 1), at]
            classes = lax.broadcasted_iota(jnp.int32, (NCLASS, size), 0)
            onehots.append(jnp.where(classes == named, 1.0, 0.0).astype(jnp.bfloat16))
            scores.append(lax.dot_general(queries, keys, NT, preferred_element_type=jnp.float32))
        scores = jnp.concatenate(scores, axis=1)
        m_old = m_s[p]
        m_new = jnp.maximum(m_old, jnp.max(scores, axis=1, keepdims=True))
        m_s[p] = m_new
        fade = jnp.exp2((m_old - m_new) * log2e)
        wide = jnp.concatenate([m_new] * (scores.shape[1] // 128), axis=1)
        weights = jnp.exp2((scores - wide) * log2e)
        high = weights.astype(jnp.bfloat16)
        low = (weights - high.astype(jnp.float32)).astype(jnp.bfloat16)
        sums = lax.dot_general(
            jnp.concatenate([high, low], axis=1), jnp.concatenate(onehots * 2, axis=1), NT,
            preferred_element_type=jnp.float32,
        )
        acc[p] = acc[p] * fade + sums

    def own_unit(t, carry):
        p, i = lax.div(t, 2), lax.rem(t, 2)
        col = lax.rem(c + i, 2)
        pl.when(t == 2)(lambda: event(3))
        pl.when(t == 3)(lambda: event(4))

        @pl.when(i == 1)
        def _():
            ref = kbuf.at[p, x * 2 + col]
            pltpu.make_async_copy(ref, ref, so_r.at[p]).wait()

        unit(p, [(p, x, col, quarter) for quarter in range(4)])
        return carry

    def passed(g):
        for way in range(2):
            ref = piece(*landed(way, g, 1 - c))
            pltpu.make_async_copy(ref, ref, bs_r.at[way, g]).wait()

    def ring_unit(g, carry):
        for at, turn in ((0, 5), (3, 6), (5, 7), (7, 8), (8, 9), (9, 10)):
            pl.when(g == at)(functools.partial(event, turn))

        passed(g)
        unit(lax.div(g, 6), [landed(way, g, col) for col in (c, 1 - c) for way in range(2)])
        return carry

    def late_unit(t, carry):
        g, i = 10 + lax.div(t, 2), lax.rem(t, 2)

        @pl.when(t == 1)
        def _():
            last_event(0)
            passed(g)

        pl.when(t == 2)(lambda: last_event(1))
        unit(PARTS - 1, [landed(way, g, lax.rem(c + i, 2)) for way in range(2)])
        return carry

    def last_unit(j, carry):
        for way in range(2):
            p, xx, col, quarter = landed(way, 11, 1 - c)
            start = pl.multiple_of(quarter * qrows + j * hrows, hrows)
            ref = kbuf.at[p, xx * 2 + col, pl.ds(start, hrows)]
            pltpu.make_async_copy(ref, ref, lb_r.at[way, j]).wait()
        unit(PARTS - 1, [landed(way, 11, 1 - c) for way in range(2)], j)
        return carry

    def finish(p):
        lane = lax.broadcasted_iota(jnp.int32, (half, 128), 1) % CAP
        slot = lax.broadcasted_iota(jnp.int32, (half, 128), 0) % CAP
        diag = jnp.where(lane == slot, m_s[p], 0.0).reshape(nd, CAP, 128)
        mout[p, :, 0] = jnp.sum(diag, axis=1, keepdims=True)
        sums = acc[p]
        most = jnp.max(sums, axis=1, keepdims=True)
        diag = jnp.where(lane == slot, most, 0.0).reshape(nd, CAP, 128)
        mout[p, :, 1] = jnp.sum(diag, axis=1, keepdims=True)
        codes = jnp.round(sums * (STEPS / most)).astype(jnp.int32).astype(jnp.int16)
        wire[p] = codes.reshape(nd, CAP, NCLASS)

    def send_back(p):
        to_all(
            (lambda d: mout.at[p, d], lambda d: pin.at[p, d], ps.at[p], pr.at[p]),
            (lambda d: wire.at[p, d], lambda d: ret.at[p, d], rs.at[p], rr.at[p]),
        )

    event(0)
    far = pl.ds(0, nx - 1)
    pltpu.make_async_copy(lab.at[far], lab.at[far], lr).wait()
    for k in range(1, nx):
        send_label(lax.rem(x + k, nx), sibling, ms, mr)
    event(1)
    share_own(1).start()
    m_s[...] = jnp.full(m_s.shape, -3.0e38, jnp.float32)
    acc[...] = jnp.zeros(acc.shape, jnp.float32)
    mask[...] = sel.T
    few = pl.ds(0, nx)
    pltpu.make_async_copy(lab.at[few], lab.at[few], mr).wait()
    event(2)
    pltpu.make_async_copy(inbox, inbox, qr).wait()
    lax.fori_loop(0, 4, own_unit, 0)

    def whole_part(p, carry):
        lax.fori_loop(6 * p, 6 + 4 * p, ring_unit, 0)

        @pl.when(p == 1)
        def _():
            lax.fori_loop(0, 3, late_unit, 0)
            lax.fori_loop(0, 2, last_unit, 0)

        finish(p)
        send_back(p)
        return carry

    lax.fori_loop(0, PARTS, whole_part, 0)

    def gone(g, carry):
        for way in range(2):
            ring(way, g).wait_send()
            share(way, g).wait_send()
        return carry

    lax.fori_loop(0, 11, gone, 0)
    for way in range(2):
        for j in range(2):
            last_ring(way, j).wait_send()
            last_share(way, j).wait_send()
    for p in range(PARTS):
        share_own(p).wait_send()
    others = pl.ds(0, nd - 1)
    pltpu.make_async_copy(outbox.at[:, others], outbox.at[:, others], qs).wait()
    pltpu.make_async_copy(lab.at[far], lab.at[far], ls).wait()
    pltpu.make_async_copy(lab.at[few], lab.at[few], ms).wait()

    def left_home(p):
        pltpu.make_async_copy(wire.at[p, others], wire.at[p, others], rs.at[p]).wait()
        pltpu.make_async_copy(mout.at[p, others], mout.at[p, others], ps.at[p]).wait()

    left_home(0)

    nq = q_ref.shape[0]
    per = 128 // CAP
    lane = lax.broadcasted_iota(jnp.int32, (1, 128), 1) // CAP
    top = jnp.full((nq, 1), -3.0e38, jnp.float32)
    total = jnp.zeros((nq, NCLASS), jnp.float32)
    for p in range(PARTS):
        pltpu.make_async_copy(pin.at[p], pin.at[p], pr.at[p]).wait()
        found = []
        new_top = top
        for g in range(half // 128):
            line = jnp.zeros((1, 128), jnp.float32)
            most = jnp.zeros((1, 128), jnp.float32)
            for i in range(per):
                line = jnp.where(lane == i, pin[p, g * per + i, 0], line)
                most = jnp.where(lane == i, pin[p, g * per + i, 1], most)
            chosen = mask[:, p * half + g * 128 : p * half + (g + 1) * 128] > 0.0
            found.append((chosen, line, most))
            best = jnp.max(jnp.where(chosen, line, -3.0e38), axis=1, keepdims=True)
            new_top = jnp.maximum(new_top, best)
        total = total * jnp.exp2((top - new_top) * log2e)
        top = new_top
        factors = [
            jnp.where(chosen, jnp.exp2(jnp.where(chosen, line - top, 0.0) * log2e) * (most / STEPS), 0.0)
            for chosen, line, most in found
        ]
        pltpu.make_async_copy(ret.at[p], ret.at[p], rr.at[p]).wait()
        codes = ret[p].astype(jnp.int32).astype(jnp.float32).reshape(half, NCLASS)
        total += jnp.dot(
            jnp.concatenate(factors, axis=1), codes,
            precision=lax.Precision.HIGHEST, preferred_element_type=jnp.float32,
        )
    out_ref[...] = NCLASS * total / jnp.sum(total, axis=1, keepdims=True)
    left_home(1)


def local(queries, probes, corpus, labels):
    nd = lax.axis_size("dom")
    nrep = lax.axis_size("rep")
    nq, depth = queries.shape
    rows = corpus.shape[1]
    half = nd * CAP
    dma = pltpu.SemaphoreType.DMA
    return pl.pallas_call(
        functools.partial(kernel, nd, nrep // 2),
        out_shape=jax.ShapeDtypeStruct((nq, NCLASS), jnp.float32),
        in_specs=[pl.BlockSpec(memory_space=pl.ANY)] * 4,
        out_specs=pl.BlockSpec(memory_space=pltpu.VMEM),
        scratch_shapes=[
            pltpu.VMEM((nq, depth), jnp.bfloat16),
            pltpu.VMEM((probes.shape[1], nq), jnp.int32),
            pltpu.VMEM((nq, PARTS * half), jnp.float32),
            pltpu.VMEM((PARTS, nd, CAP, depth), jnp.bfloat16),
            pltpu.VMEM((PARTS, nd, CAP, depth), jnp.bfloat16),
            pltpu.VMEM((PARTS, nrep, rows, depth), jnp.bfloat16),
            pltpu.VMEM((nrep, PARTS, rows), jnp.int32),
            pltpu.VMEM((PARTS, half, NCLASS), jnp.float32),
            pltpu.VMEM((PARTS, half, 128), jnp.float32),
            pltpu.VMEM((PARTS, nd, CAP, NCLASS), jnp.int16),
            pltpu.VMEM((PARTS, nd, 2, 1, 128), jnp.float32),
            pltpu.VMEM((PARTS, nd, 2, 1, 128), jnp.float32),
            pltpu.VMEM((PARTS, nd, CAP, NCLASS), jnp.int16),
            dma((3,)),
            dma((PARTS,)),
            dma((PARTS,)),
            dma((PARTS,)),
            dma((2, 11)),
            dma((2, 11)),
            dma((2, 11)),
            dma((2, 11)),
            dma((2, 2)),
            dma((2, 2)),
            dma((2, 2)),
            dma((2, 2)),
            dma, dma, dma, dma, dma, dma,
            dma((PARTS,)),
            dma((PARTS,)),
            dma((PARTS,)),
            dma((PARTS,)),
        ],
        compiler_params=pltpu.CompilerParams(
            collective_id=0, has_side_effects=True, vmem_limit_bytes=62 * 1024 * 1024
        ),
    )(queries, probes.T, corpus, labels)


def solution(mesh):
    in_specs = (
        P(("dom", "rep"), None),
        P(("dom", "rep"), None),
        P("dom", "rep", None),
        P("dom", "rep"),
    )
    out_specs = P(("dom", "rep"), None)
    return jax.shard_map(local, mesh=mesh, in_specs=in_specs, out_specs=out_specs, check_vma=False)
```

```python
import functools
import math

import jax
import jax.numpy as jnp
from jax import lax
from jax.experimental import pallas as pl
from jax.experimental.pallas import tpu as pltpu
from jax.sharding import PartitionSpec as P

NCLASS = 128
CAP = 16
PARTS = 2
WINDOW = 4
STEPS = 32767.0
PEAK_UNIT = 2.0**-12
MOST_UNIT = 2.0**-17
MESH = pl.DeviceIdType.MESH
NT = (((1,), (1,)), ((), ()))


def select_slots(named, nd):
    npr, nq = named.shape
    nparts = PARTS * nd
    width = max(128, nparts)
    part_ids = lax.broadcasted_iota(jnp.int32, (width, nq), 0)
    match = jnp.zeros((width, nq), jnp.float32)
    for j in range(npr):
        match = jnp.where(named[j : j + 1, :] == part_ids, 1.0, match)
    row = lax.broadcasted_iota(jnp.int32, (nq, nq), 0)
    col = lax.broadcasted_iota(jnp.int32, (nq, nq), 1)
    earlier = jnp.where(row < col, 1.0, 0.0).astype(jnp.bfloat16)
    rank = jnp.dot(match.astype(jnp.bfloat16), earlier, preferred_element_type=jnp.float32)
    code = jnp.where(match > 0.0, rank, -1.0)
    slots = nparts * CAP
    half = nd * CAP
    slot_row = lax.broadcasted_iota(jnp.int32, (slots, width), 0)
    slot_part = PARTS * ((slot_row % half) // CAP) + slot_row // half
    spread = jnp.where(lax.broadcasted_iota(jnp.int32, (slots, width), 1) == slot_part, 1.0, 0.0)
    wide = jnp.dot(
        spread.astype(jnp.bfloat16), code.astype(jnp.bfloat16), preferred_element_type=jnp.float32
    )
    slot = (lax.broadcasted_iota(jnp.int32, (slots, nq), 0) % CAP).astype(jnp.float32)
    return jnp.where(wide == slot, 1.0, 0.0)


def kernel(
    nd, nx,
    q_hbm, probes_hbm, corpus_hbm, labels_hbm, out_ref,
    q_ref, probes_ref, mask, outbox, inbox, kbuf, lab, acc, m_s, wire, ret,
    fs, ko, so_s, so_r, ks, kr, bs_s, bs_r, ls_s, ls_r, lb_s, lb_r, qs, qr, ls, lr, ms, mr, rs, rr,
):
    dom = lax.axis_index("dom")
    rep = lax.axis_index("rep")
    x, c = lax.div(rep, 2), lax.rem(rep, 2)
    rows = kbuf.shape[2]
    qrows = rows // 4
    hrows = rows // 8
    half = nd * CAP
    nz = min(nd, 8)
    ny = nd // nz
    y, z = lax.div(dom, nz), lax.rem(dom, nz)
    right = (dom, lax.rem(x + 1, nx) * 2 + c)
    left = (dom, lax.rem(x + nx - 1, nx) * 2 + c)
    across = (dom, lax.rem(x + 2, nx) * 2 + c)
    sibling = (dom, x * 2 + (1 - c))

    lines = [
        lax.rem(y + (ny // 2 + (1 - 2 * (j % 2)) * ((j + 1) // 2)), ny) * nz for j in range(ny)
    ]

    def each_peer(act):
        def one(i, carry):
            dz = nz // 2 + (1 - 2 * lax.rem(i, 2)) * lax.div(i + 1, 2)
            there = lax.rem(z + dz, nz)
            for line in lines:
                act(line + there)
            return carry

        lax.fori_loop(0, nz - 1, one, 0)
        for line in lines[:-1]:
            act(line + z)

    barrier = pltpu.get_barrier_semaphore()

    def greet(device):
        pl.semaphore_signal(barrier, inc=1, device_id=device, device_id_type=MESH)

    for device in (sibling, right, left, across):
        greet(device)
    each_peer(lambda peer: greet((peer, rep)))

    get_probes = pltpu.make_async_copy(probes_hbm, probes_ref, fs.at[0])
    get_queries = pltpu.make_async_copy(q_hbm, q_ref, fs.at[1])
    get_labels = pltpu.make_async_copy(labels_hbm, lab.at[rep], fs.at[2])
    get_rows = [
        pltpu.make_async_copy(corpus_hbm.at[p], kbuf.at[p, rep], ko.at[p]) for p in range(PARTS)
    ]
    for copy in (get_probes, get_queries, get_rows[0], get_labels, get_rows[1]):
        copy.start()
    get_rows[0].wait()

    pl.semaphore_wait(barrier, nd + 3)

    def piece(p, xx, col, quarter):
        return kbuf.at[p, xx * 2 + col, pl.ds(pl.multiple_of(quarter * qrows, qrows), qrows)]

    def ring(way, g):
        p, k = lax.div(g, 6), lax.rem(g, 6)
        if way == 0:
            ref = piece(p, lax.rem(x + nx - lax.div(k, 4), nx), c, lax.rem(k, 4))
        else:
            ref = piece(p, lax.rem(x + lax.div(k, 4), nx), c, 3 - lax.rem(k, 4))
        return pltpu.make_async_remote_copy(
            src_ref=ref, dst_ref=ref, send_sem=ks.at[way, g], recv_sem=kr.at[way, g],
            device_id=right if way == 0 else left, device_id_type=MESH,
        )

    def landed(way, g, col):
        p, k = lax.div(g, 6), lax.rem(g, 6)
        if way == 0:
            return p, lax.rem(x + 2 * nx - 1 - lax.div(k, 4), nx), col, lax.rem(k, 4)
        return p, lax.rem(x + 1 + lax.div(k, 4), nx), col, 3 - lax.rem(k, 4)

    def share(way, g):
        ref = piece(*landed(way, g, c))
        return pltpu.make_async_remote_copy(
            src_ref=ref, dst_ref=ref, send_sem=bs_s.at[way, g], recv_sem=bs_r.at[way, g],
            device_id=sibling, device_id_type=MESH,
        )

    def halves(way, col):
        p, xx, col, quarter = landed(way, 11, col)
        return [
            kbuf.at[p, xx * 2 + col, pl.ds(pl.multiple_of(quarter * qrows + j * hrows, hrows), hrows)]
            for j in range(2)
        ]

    def last_ring(way, j):
        p, xx, quarter = PARTS - 1, lax.rem(x + (nx - 1 if way == 0 else 1), nx), 1 if way == 0 else 2
        ref = kbuf.at[p, xx * 2 + c, pl.ds(quarter * qrows + j * hrows, hrows)]
        return pltpu.make_async_remote_copy(
            src_ref=ref, dst_ref=ref, send_sem=ls_s.at[way, j], recv_sem=ls_r.at[way, j],
            device_id=right if way == 0 else left, device_id_type=MESH,
        )

    def last_share(way, j):
        ref = halves(way, c)[j]
        return pltpu.make_async_remote_copy(
            src_ref=ref, dst_ref=ref, send_sem=lb_s.at[way, j], recv_sem=lb_r.at[way, j],
            device_id=sibling, device_id_type=MESH,
        )

    def share_own(p):
        ref = kbuf.at[p, rep]
        return pltpu.make_async_remote_copy(
            src_ref=ref, dst_ref=ref, send_sem=so_s.at[p], recv_sem=so_r.at[p],
            device_id=sibling, device_id_type=MESH,
        )

    for g in range(WINDOW):
        ring(0, g).start()
        ring(1, g).start()

    get_probes.wait()
    get_queries.wait()
    sel = select_slots(probes_ref[...], nd)
    picked = jnp.dot(sel.astype(jnp.bfloat16), q_ref[...], preferred_element_type=jnp.float32)
    outbox[...] = picked.astype(jnp.bfloat16).reshape(outbox.shape)
    get_labels.wait()
    get_rows[1].wait()


    def to_all(*blocks):
        def send(peer):
            for src, dst, send_sem, recv_sem in blocks:
                pltpu.make_async_remote_copy(
                    src_ref=src(peer), dst_ref=dst(dom), send_sem=send_sem, recv_sem=recv_sem,
                    device_id=(peer, rep), device_id_type=MESH,
                ).start()

        each_peer(send)
        for src, dst, _, recv_sem in blocks:
            pltpu.make_async_copy(src(dom), dst(dom), recv_sem).start()

    to_all((lambda d: outbox.at[:, d], lambda d: inbox.at[:, d], qs, qr))

    def send_label(xx, device, send_sem, recv_sem):
        ref = lab.at[xx * 2 + c]
        pltpu.make_async_remote_copy(
            src_ref=ref, dst_ref=ref, send_sem=send_sem, recv_sem=recv_sem,
            device_id=device, device_id_type=MESH,
        ).start()

    for device in (right, left, across):
        send_label(x, device, ls, lr)
    send_label(x, sibling, ms, mr)
    share_own(0).start()

    def event(g):
        for way in range(2):
            ref = piece(*landed(way, g, c))
            pltpu.make_async_copy(ref, ref, kr.at[way, g]).wait()
            share(way, g).start()

        for way in range(2):
            if g + WINDOW < 11:
                ring(way, g + WINDOW).start()
            elif g + WINDOW == 11:
                last_ring(way, 0).start()
                last_ring(way, 1).start()

    def last_event(j):
        for way in range(2):
            ref = halves(way, c)[j]
            pltpu.make_async_copy(ref, ref, ls_r.at[way, j]).wait()
            last_share(way, j).start()

    log2e = math.log2(math.e) * (q_ref.shape[1] ** -0.5)

    def unit(p, pieces, cut=None):
        queries = inbox[p].reshape(half, -1)
        scores, onehots = [], []
        for _, xx, col, quarter in pieces:
            size, start = qrows, quarter * qrows
            if cut is not None:
                size, start = hrows, start + cut * hrows
            at = pl.ds(pl.multiple_of(start, size), size)
            keys = kbuf[p, xx * 2 + col, at, :]
            named = lab[xx * 2 + col, pl.ds(p, 1), at]
            classes = lax.broadcasted_iota(jnp.int32, (NCLASS, size), 0)
            onehots.append(jnp.where(classes == named, 1.0, 0.0).astype(jnp.bfloat16))
            scores.append(lax.dot_general(queries, keys, NT, preferred_element_type=jnp.float32))
        scores = jnp.concatenate(scores, axis=1)
        m_old = m_s[p]
        m_new = jnp.maximum(m_old, jnp.max(scores, axis=1, keepdims=True))
        m_s[p] = m_new
        fade = jnp.exp2((m_old - m_new) * log2e)
        wide = jnp.concatenate([m_new] * (scores.shape[1] // 128), axis=1)
        weights = jnp.exp2((scores - wide) * log2e)
        high = weights.astype(jnp.bfloat16)
        low = (weights - high.astype(jnp.float32)).astype(jnp.bfloat16)
        sums = lax.dot_general(
            jnp.concatenate([high, low], axis=1), jnp.concatenate(onehots * 2, axis=1), NT,
            preferred_element_type=jnp.float32,
        )
        acc[p] = acc[p] * fade + sums

    def own_unit(t, carry):
        p, i = lax.div(t, 2), lax.rem(t, 2)
        col = lax.rem(c + i, 2)
        pl.when(t == 2)(lambda: event(3))
        pl.when(t == 3)(lambda: event(4))

        @pl.when(i == 1)
        def _():
            ref = kbuf.at[p, x * 2 + col]
            pltpu.make_async_copy(ref, ref, so_r.at[p]).wait()

        unit(p, [(p, x, col, quarter) for quarter in range(4)])
        return carry

    def passed(g):
        for way in range(2):
            ref = piece(*landed(way, g, 1 - c))
            pltpu.make_async_copy(ref, ref, bs_r.at[way, g]).wait()

    def ring_unit(g, carry):
        for at, turn in ((0, 5), (3, 6), (5, 7), (7, 8), (8, 9), (9, 10)):
            pl.when(g == at)(functools.partial(event, turn))

        passed(g)
        unit(lax.div(g, 6), [landed(way, g, col) for col in (c, 1 - c) for way in range(2)])
        return carry

    def late_unit(t, carry):
        g, i = 10 + lax.div(t, 2), lax.rem(t, 2)

        @pl.when(t == 1)
        def _():
            last_event(0)
            passed(g)

        pl.when(t == 2)(lambda: last_event(1))
        unit(PARTS - 1, [landed(way, g, lax.rem(c + i, 2)) for way in range(2)])
        return carry

    def last_unit(j, carry):
        for way in range(2):
            p, xx, col, quarter = landed(way, 11, 1 - c)
            start = pl.multiple_of(quarter * qrows + j * hrows, hrows)
            ref = kbuf.at[p, xx * 2 + col, pl.ds(start, hrows)]
            pltpu.make_async_copy(ref, ref, lb_r.at[way, j]).wait()
        unit(PARTS - 1, [landed(way, 11, 1 - c) for way in range(2)], j)
        return carry

    def finish(p):
        lane = lax.broadcasted_iota(jnp.int32, (half, 128), 1) % CAP
        slot = lax.broadcasted_iota(jnp.int32, (half, 128), 0) % CAP
        diag = jnp.where(lane == slot, m_s[p], 0.0).reshape(nd, CAP, 128)
        peaks = jnp.sum(diag, axis=1, keepdims=True)
        sums = acc[p]
        most = jnp.max(sums, axis=1, keepdims=True)
        most = (most * (1.0 / MOST_UNIT)).astype(jnp.int32) + 1
        diag = jnp.where(lane == slot, most, 0).reshape(nd, CAP, 128)
        wire[p, :, 8:9] = jnp.round(peaks * (1.0 / PEAK_UNIT)).astype(jnp.int32)
        wire[p, :, 9:10] = jnp.sum(diag, axis=1, keepdims=True)
        codes = jnp.round(sums * (STEPS / (most.astype(jnp.float32) * MOST_UNIT))).astype(jnp.int32)
        codes = codes.reshape(nd, CAP, NCLASS)
        wire[p, :, 0:8] = codes[:, :8] * 65536 + codes[:, 8:]

    def send_back(p):
        to_all(
            (lambda d: wire.at[p, d], lambda d: ret.at[p, d], rs.at[p], rr.at[p]),
        )

    event(0)
    far = pl.ds(0, nx - 1)
    pltpu.make_async_copy(lab.at[far], lab.at[far], lr).wait()
    for k in range(1, nx):
        send_label(lax.rem(x + k, nx), sibling, ms, mr)
    event(1)
    share_own(1).start()
    m_s[...] = jnp.full(m_s.shape, -3.0e38, jnp.float32)
    acc[...] = jnp.zeros(acc.shape, jnp.float32)
    mask[...] = sel.T
    few = pl.ds(0, nx)
    pltpu.make_async_copy(lab.at[few], lab.at[few], mr).wait()
    event(2)
    pltpu.make_async_copy(inbox, inbox, qr).wait()
    lax.fori_loop(0, 4, own_unit, 0)

    def whole_part(p, carry):
        lax.fori_loop(6 * p, 6 + 4 * p, ring_unit, 0)

        @pl.when(p == 1)
        def _():
            lax.fori_loop(0, 3, late_unit, 0)
            lax.fori_loop(0, 2, last_unit, 0)

        finish(p)
        send_back(p)
        return carry

    lax.fori_loop(0, PARTS, whole_part, 0)

    def gone(g, carry):
        for way in range(2):
            ring(way, g).wait_send()
            share(way, g).wait_send()
        return carry

    lax.fori_loop(0, 11, gone, 0)
    for way in range(2):
        for j in range(2):
            last_ring(way, j).wait_send()
            last_share(way, j).wait_send()
    for p in range(PARTS):
        share_own(p).wait_send()
    others = pl.ds(0, nd - 1)
    pltpu.make_async_copy(outbox.at[:, others], outbox.at[:, others], qs).wait()
    pltpu.make_async_copy(lab.at[far], lab.at[far], ls).wait()
    pltpu.make_async_copy(lab.at[few], lab.at[few], ms).wait()

    def left_home(p):
        pltpu.make_async_copy(wire.at[p, others], wire.at[p, others], rs.at[p]).wait()

    left_home(0)

    nq = q_ref.shape[0]
    per = 128 // CAP
    lane = lax.broadcasted_iota(jnp.int32, (1, 128), 1) // CAP
    top = jnp.full((nq, 1), -3.0e38, jnp.float32)
    total = jnp.zeros((nq, NCLASS), jnp.float32)
    for p in range(PARTS):
        pltpu.make_async_copy(ret.at[p], ret.at[p], rr.at[p]).wait()
        found = []
        new_top = top
        for g in range(half // 128):
            line = jnp.zeros((1, 128), jnp.int32)
            most = jnp.zeros((1, 128), jnp.int32)
            for i in range(per):
                line = jnp.where(lane == i, ret[p, g * per + i, 8:9], line)
                most = jnp.where(lane == i, ret[p, g * per + i, 9:10], most)
            line = line.astype(jnp.float32) * PEAK_UNIT
            most = most.astype(jnp.float32) * MOST_UNIT
            chosen = mask[:, p * half + g * 128 : p * half + (g + 1) * 128] > 0.0
            found.append((chosen, line, most))
            best = jnp.max(jnp.where(chosen, line, -3.0e38), axis=1, keepdims=True)
            new_top = jnp.maximum(new_top, best)
        total = total * jnp.exp2((top - new_top) * log2e)
        top = new_top
        factors = [
            jnp.where(chosen, jnp.exp2(jnp.where(chosen, line - top, 0.0) * log2e) * (most / STEPS), 0.0)
            for chosen, line, most in found
        ]
        pairs = ret[p, :, 0:8]
        codes = jnp.concatenate([lax.shift_right_logical(pairs, 16), pairs & 65535], axis=1)
        codes = codes.astype(jnp.float32).reshape(half, NCLASS)
        total += jnp.dot(
            jnp.concatenate(factors, axis=1), codes,
            precision=lax.Precision.HIGHEST, preferred_element_type=jnp.float32,
        )
    out_ref[...] = NCLASS * total / jnp.sum(total, axis=1, keepdims=True)
    left_home(1)


def local(queries, probes, corpus, labels):
    nd = lax.axis_size("dom")
    nrep = lax.axis_size("rep")
    nq, depth = queries.shape
    rows = corpus.shape[1]
    half = nd * CAP
    dma = pltpu.SemaphoreType.DMA
    return pl.pallas_call(
        functools.partial(kernel, nd, nrep // 2),
        out_shape=jax.ShapeDtypeStruct((nq, NCLASS), jnp.float32),
        in_specs=[pl.BlockSpec(memory_space=pl.ANY)] * 4,
        out_specs=pl.BlockSpec(memory_space=pltpu.VMEM),
        scratch_shapes=[
            pltpu.VMEM((nq, depth), jnp.bfloat16),
            pltpu.VMEM((probes.shape[1], nq), jnp.int32),
            pltpu.VMEM((nq, PARTS * half), jnp.float32),
            pltpu.VMEM((PARTS, nd, CAP, depth), jnp.bfloat16),
            pltpu.VMEM((PARTS, nd, CAP, depth), jnp.bfloat16),
            pltpu.VMEM((PARTS, nrep, rows, depth), jnp.bfloat16),
            pltpu.VMEM((nrep, PARTS, rows), jnp.int32),
            pltpu.VMEM((PARTS, half, NCLASS), jnp.float32),
            pltpu.VMEM((PARTS, half, 128), jnp.float32),
            pltpu.VMEM((PARTS, nd, 10, NCLASS), jnp.int32),
            pltpu.VMEM((PARTS, nd, 10, NCLASS), jnp.int32),
            dma((3,)),
            dma((PARTS,)),
            dma((PARTS,)),
            dma((PARTS,)),
            dma((2, 11)),
            dma((2, 11)),
            dma((2, 11)),
            dma((2, 11)),
            dma((2, 2)),
            dma((2, 2)),
            dma((2, 2)),
            dma((2, 2)),
            dma, dma, dma, dma, dma, dma,
            dma((PARTS,)),
            dma((PARTS,)),
        ],
        compiler_params=pltpu.CompilerParams(
            collective_id=0, has_side_effects=True, vmem_limit_bytes=62 * 1024 * 1024
        ),
    )(queries, probes.T, corpus, labels)


def solution(mesh):
    in_specs = (
        P(("dom", "rep"), None),
        P(("dom", "rep"), None),
        P("dom", "rep", None),
        P("dom", "rep"),
    )
    out_specs = P(("dom", "rep"), None)
    return jax.shard_map(local, mesh=mesh, in_specs=in_specs, out_specs=out_specs, check_vma=False)
```
